32 devices in a mesh: sta: 16 (over z, y, x), tm: 2 (over core).
Axes of the slice: x: 2, y: 2, z: 4, core: 2. Of those that a mesh axis runs over, the one named last changes fastest.
Arguments:
- strain: bfloat16 [24000, 4096], P('tm', 'sta')
- masks: int32 [2], replicated, may hold values from 1 to 15, as said below
- pair_local: int32 [2, 4096], P(None, 'sta'), may hold values from 0 to 255
- pair_remote: int32 [2, 4096], P(None, 'sta'), may hold values from 0 to 255
- owner: int32 [8192, 1], P('sta'), may hold values from 0 to 15; in each aligned block of 512 rows (0 to 511, 512 to 1023, ...) at most 64 rows name the same one
Outputs:
- correlations: float32 [16384, 512], P('sta', 'tm')
The draws below stay inside these ranges and needn't reach their ends.
Inputs may be any that keep to these rules, and one draw needn't show every extreme that they name: `masks`: the 2 entries are distinct, and one of them is 15. At most 64 of the 512 pairs of one station group have the same owner.
All inputs are finite; a program needn't handle non-finite values.
Results may differ from the reference program's by a relative error of at most 0.0051.
Values may be sent and summed in bfloat16 or wider, within the bound.
A program may use at most 64 MiB of HBM per device.

```python
import math
import jax
import jax.numpy as jnp
import numpy as np
from jax import lax

CH_DEV = 256
SEG_LEN = 6000
SEGS_DEV = 2
FREQS = 512
WIN = 32
LAGS = 512
ROUNDS = 2
PAIRS = 256
CAP = 64
CHANNELS = 4096
SAMPLES = 24000
N_STA = 16
N_TM = 2


def draw_strain(key, part):
    keys = jax.random.split(key, 5)
    channel_scale = jnp.exp(jax.random.uniform(keys[0], (CHANNELS,), jnp.float32, 0.0, math.log(10.0)))
    noise = jax.random.normal(keys[1], (SAMPLES, CHANNELS), jnp.float32)
    tone_size = jax.random.uniform(keys[4], (CHANNELS,), jnp.float32, 0.02, 0.2)
    tone_bin = jax.random.randint(keys[2], (CHANNELS,), 1, FREQS + 1, dtype=jnp.int32)
    tone_shift = jax.random.randint(keys[3], (CHANNELS,), 0, SEG_LEN, dtype=jnp.int32)
    sample_index = jnp.arange(SAMPLES, dtype=jnp.int32)[:, None]
    angles = jnp.mod(tone_bin[None, :] * sample_index + tone_shift[None, :], SEG_LEN).astype(jnp.float32) * jnp.float32(2.0 * math.pi / SEG_LEN)
    return (channel_scale[None, :] * (noise + tone_size[None, :] * jnp.cos(angles))).astype(jnp.bfloat16)


def draw_masks(key, part):
    first_key, order_key = jax.random.split(key)
    others = jax.random.permutation(first_key, N_STA - 2)[:ROUNDS - 1] + 1
    full_mask = jnp.full((1,), N_STA - 1, dtype=jnp.int32)
    joined = jnp.concatenate([full_mask, others.astype(jnp.int32)], axis=0)
    return jax.random.permutation(order_key, joined).astype(jnp.int32)


def place_ends(drawn, key, smallest, top_value):
    extent = drawn.shape
    place = [jax.random.randint(jax.random.fold_in(key, axis), (), 0, extent[axis]) for axis in range(len(extent))]
    drawn = drawn.at[tuple(place)].set(smallest)
    longest = extent.index(max(extent))
    place[longest] = (place[longest] + 1) % extent[longest]
    return drawn.at[tuple(place)].set(top_value)


def assign_block(rng, own, number, rows, amount, top, reach, skew):
    ranking = jax.random.permutation(rng, amount)
    heavy_load, ordinary = portions_of(amount, rows * top, reach, skew, True), portions_of(amount, rows * top, reach, skew, False)
    places = jnp.arange(amount)

    def named(sizes, turn):
        used = int((sizes > 0).sum())
        fixed = max(1, used // 4)
        passed = fixed + (places - fixed + turn * (used - fixed)) % max(1, amount - fixed)
        return jnp.zeros((amount,), jnp.int32).at[ranking[jnp.where(places < fixed, places, passed)]].set(jnp.asarray(sizes, jnp.int32))

    sizes = jnp.where(number % 4 == 0, named(heavy_load, number // 4), named(ordinary, number - number // 4 - 1))
    mixed = jax.random.permutation(jax.random.fold_in(own, 3), amount)
    giver, sink = mixed[0:amount // 2 * 2:2], mixed[1:amount // 2 * 2:2]
    margin = jnp.minimum(sizes[giver] - 1, reach - sizes[sink]) // 2
    margin = jnp.where((giver == ranking[0]) | (sink == ranking[0]) | (sizes[sink] == 0), 0, jnp.maximum(margin, 0))
    passed = jax.random.randint(jax.random.fold_in(own, 4), (amount // 2,), 0, 1 << 20) % (margin + 1)
    sizes = sizes.at[giver].add(-passed).at[sink].add(passed)
    members = jnp.searchsorted(jnp.cumsum(sizes), jnp.arange(rows * top), side="right").astype(jnp.int32)
    listing = members.reshape(top, rows).T
    listing = listing[jax.random.permutation(jax.random.fold_in(own, 1), rows)]
    turn = jax.random.randint(jax.random.fold_in(own, 2), (rows, 1), 0, top)
    return jnp.take_along_axis(listing, (jnp.arange(top)[None, :] + turn) % top, axis=1)


def portions_of(amount, total, bound, lean, full):
    loads = [(1 << 20) // math.isqrt(grade ** lean) + 1 for grade in range(1, amount + 1)]
    largest = bound if full else min(bound, max(-(-total // amount), total * loads[0] // sum(loads)))
    least = 1 if total - largest >= amount - 1 else 0
    holding, spare = [largest] + [least] * (amount - 1), total - largest - least * (amount - 1)
    while spare > 0:
        movable = [i for i in range(1, amount) if holding[i] < largest] or [i for i in range(1, amount) if holding[i] < bound]
        whole, left = sum([loads[i] for i in movable]), spare
        for i in movable:
            addition = min(bound - holding[i], max(1, left * loads[i] // whole), spare)
            holding[i] = holding[i] + addition
            spare = spare - addition
    return np.array(holding)


def setup_inputs(seed: int = 0) -> dict:
    key_list = jax.random.split(jax.random.key(seed), 6)
    strain = draw_strain(jax.random.fold_in(key_list[5], 71), 0)
    masks = draw_masks(jax.random.fold_in(key_list[5], 71), 0)
    pair_local = place_ends(jax.random.randint(key_list[2], (ROUNDS, N_STA * PAIRS), 0, CH_DEV), jax.random.fold_in(key_list[2], 1), 0, CH_DEV - 1).astype(jnp.int32)
    pair_remote = place_ends(jax.random.randint(key_list[3], (ROUNDS, N_STA * PAIRS), 0, CH_DEV), jax.random.fold_in(key_list[3], 1), 0, CH_DEV - 1).astype(jnp.int32)
    owner_keys = jax.random.split(jax.random.fold_in(key_list[4], 1), (N_STA * ROUNDS * PAIRS) // (ROUNDS * PAIRS))
    owner_turns = jax.random.permutation(jax.random.fold_in(key_list[4], 3), (N_STA * ROUNDS * PAIRS) // (ROUNDS * PAIRS))
    owner = jax.vmap(lambda own, number: assign_block(jax.random.fold_in(key_list[4], 2), own, number, ROUNDS * PAIRS, N_STA, 1, CAP, 2))(owner_keys, owner_turns).reshape((N_STA * ROUNDS * PAIRS, 1))
    return {"strain": strain, "masks": masks, "pair_local": pair_local, "pair_remote": pair_remote, "owner": owner}


EPSILON = 1e-06

def forward_table():
    freq_bins = (jnp.arange(FREQS, dtype=jnp.int32) + 1)[:, None]
    sample_index = jnp.arange(SEG_LEN, dtype=jnp.int32)[None, :]
    angles = jnp.mod(freq_bins * sample_index, SEG_LEN).astype(jnp.float32) * jnp.float32(2.0 * math.pi / SEG_LEN)
    return jnp.concatenate([jnp.cos(angles), -jnp.sin(angles)], axis=0).astype(jnp.bfloat16)

def inverse_table(first_lag, lag_count):
    freq_bins = (jnp.arange(FREQS, dtype=jnp.int32) + 1)[:, None]
    lag_index = first_lag + jnp.arange(lag_count, dtype=jnp.int32)[None, :] - LAGS // 2
    angles = jnp.mod(freq_bins * lag_index, SEG_LEN).astype(jnp.float32) * jnp.float32(2.0 * math.pi / SEG_LEN)
    return jnp.concatenate([jnp.cos(angles), -jnp.sin(angles)], axis=0)

def band_table():
    row_index = jnp.arange(FREQS, dtype=jnp.int32)[:, None]
    col_index = jnp.arange(FREQS, dtype=jnp.int32)[None, :]
    within = jnp.abs(row_index - col_index) <= WIN
    return jnp.where(within, jnp.float32(1.0 / (2 * WIN + 1)), jnp.float32(0.0))

def whiten(spectra):
    real_part = spectra[:, :FREQS]
    imag_part = spectra[:, FREQS:]
    amplitude = jnp.sqrt(real_part * real_part + imag_part * imag_part)
    smoothed = jnp.einsum('jk,sjc->skc', band_table(), amplitude, precision=lax.Precision.HIGHEST)
    divisor = jnp.concatenate([smoothed, smoothed], axis=1) + EPSILON
    return (spectra / divisor).astype(jnp.bfloat16)

def cross_rows(own_block, peer_block, local_index, remote_index):
    own_rows = jnp.take(own_block, local_index, axis=2).astype(jnp.float32)
    peer_rows = jnp.take(peer_block, remote_index, axis=2).astype(jnp.float32)
    own_real, own_imag = (own_rows[:, :FREQS], own_rows[:, FREQS:])
    peer_real, peer_imag = (peer_rows[:, :FREQS], peer_rows[:, FREQS:])
    real_sum = lax.optimization_barrier(jnp.sum(own_real * peer_real + own_imag * peer_imag, axis=0))
    imag_sum = lax.optimization_barrier(jnp.sum(own_imag * peer_real - own_real * peer_imag, axis=0))
    return jnp.concatenate([real_sum, imag_sum], axis=0).T

def slots_of(owners, slot_count):
    one_hot = (owners[:, None] == jnp.arange(slot_count, dtype=jnp.int32)[None, :]).astype(jnp.int32)
    earlier = jnp.cumsum(one_hot, axis=0) - one_hot
    return lax.optimization_barrier(jnp.sum(earlier * one_hot, axis=1)).astype(jnp.int32)

def reference(strain, masks, pair_local, pair_remote, owner):
    forward = forward_table().astype(jnp.float32)
    seg_total = SEGS_DEV * N_TM

    def group_spectra(group):
        block = lax.dynamic_slice_in_dim(strain, (group * CH_DEV).astype(jnp.int32), CH_DEV, axis=1).astype(jnp.float32)
        segments = block.reshape(seg_total, SEG_LEN, CH_DEV)
        spectra = jnp.einsum('kl,slc->skc', forward, segments, precision=lax.Precision.HIGHEST)
        return whiten(spectra)
    whitened_all = lax.map(group_spectra, jnp.arange(N_STA, dtype=jnp.int32))
    inverse = inverse_table(jnp.int32(0), LAGS)
    norm_scale = 1.0 / math.sqrt(seg_total * FREQS)

    def group_rows(group):
        rows_list = []
        for round_index in range(ROUNDS):
            partner = jnp.bitwise_xor(group, masks[round_index]).astype(jnp.int32)
            local_index = lax.dynamic_slice_in_dim(pair_local[round_index], (group * PAIRS).astype(jnp.int32), PAIRS)
            remote_index = lax.dynamic_slice_in_dim(pair_remote[round_index], (group * PAIRS).astype(jnp.int32), PAIRS)
            rows_list.append(cross_rows(whitened_all[group], whitened_all[partner], local_index, remote_index))
        pair_rows = jnp.concatenate(rows_list, axis=0)
        lagged = jnp.dot(pair_rows, inverse, precision=lax.Precision.HIGHEST) * norm_scale
        owners = lax.dynamic_slice_in_dim(owner[:, 0], (group * ROUNDS * PAIRS).astype(jnp.int32), ROUNDS * PAIRS)
        targets = owners * (N_STA * CAP) + group * CAP + slots_of(owners, N_STA)
        return (lagged, targets.astype(jnp.int32))
    lagged_all, targets_all = lax.map(group_rows, jnp.arange(N_STA, dtype=jnp.int32))
    result = jnp.zeros((N_STA * N_STA * CAP, LAGS), jnp.float32)
    return result.at[targets_all.reshape(-1)].set(lagged_all.reshape(-1, LAGS))
```

```python
import functools
import math

import jax
import jax.numpy as jnp
import ml_dtypes
import numpy as np
from jax import lax
from jax.experimental import pallas as pl
from jax.experimental.pallas import tpu as pltpu
from jax.sharding import PartitionSpec as P

SEG_LEN = 6000
SEG_PAD = 6144
FREQS = 512
WIN = 32
LAGS = 512
EPSILON = 1e-06
BLOCK = 64
BLOCKS = FREQS // BLOCK
CHUNK = 256
COEFS = 16
F32 = jnp.float32
BF16 = jnp.bfloat16
MESH = pl.DeviceIdType.MESH


def angles_of(product):
    return np.mod(product, SEG_LEN).astype(np.float32) * np.float32(2.0 * math.pi / SEG_LEN)


def forward_blocks():
    angles = angles_of(np.arange(1, FREQS + 1)[:, None] * np.arange(SEG_LEN)[None, :])
    table = np.zeros((BLOCKS, 2, BLOCK, SEG_PAD), np.float32)
    table[:, 0, :, :SEG_LEN] = np.cos(angles).reshape(BLOCKS, BLOCK, SEG_LEN)
    table[:, 1, :, :SEG_LEN] = -np.sin(angles).reshape(BLOCKS, BLOCK, SEG_LEN)
    return table.reshape(BLOCKS, 2 * BLOCK, SEG_PAD).astype(ml_dtypes.bfloat16)


def inverse_factors(slices, scale):
    angles = angles_of(np.arange(1, FREQS + 1)[:, None] * (np.arange(LAGS) - LAGS // 2)[None, :])
    angles = angles.astype(np.float64)
    bins = FREQS // slices
    left, right = [], []
    for number in range(slices):
        part = angles[number * bins : (number + 1) * bins]
        u, s, vt = np.linalg.svd(np.concatenate([np.cos(part), -np.sin(part)]), full_matrices=False)
        left.append(u[:, :COEFS].T)
        right.append(s[:COEFS, None] * vt[:COEFS] * scale)
    left = np.stack(left).astype(np.float32)
    high = left.astype(ml_dtypes.bfloat16)
    low = (left - high.astype(np.float32)).astype(ml_dtypes.bfloat16)
    return np.concatenate([high, low], axis=1), np.concatenate(right).astype(ml_dtypes.bfloat16)


def dot(left, right):
    return jnp.dot(left, right, preferred_element_type=F32)


def main_kernel(
    group_count, capacity, seg_count, pair_shape,
    strain_hbm, table_hbm, left_ref, local_ref, remote_ref, owner_ref, masks_ref,
    out_ref,
    strain_buf, table_buf, spec_buf, high_buf, low_buf, iota_buf, sent_buf, got_buf,
    index_out, index_buf, part_buf, sum_in, res_buf,
    strain_sem, table_sem, send_sem, recv_sem, isend_sem, irecv_sem,
    psend_sem, precv_sem, rsend_sem, rrecv_sem, fsend_sem, frecv_sem, own_sem,
):
    round_count, pair_count = pair_shape
    pairs = round_count * pair_count
    bins = FREQS // group_count
    per_block = BLOCK // bins
    rows = 2 * bins
    slots = group_count * capacity
    chunks = slots // CHUNK
    channels = strain_hbm.shape[1]
    me, core = lax.axis_index("sta"), lax.axis_index("tm")
    upper = me >= group_count // 2

    strain_copy = pltpu.make_async_copy(
        strain_hbm, strain_buf.at[pl.ds(0, seg_count * SEG_LEN)], strain_sem
    )
    strain_copy.start()

    def block_of(step):
        return jnp.where(upper, step, BLOCKS - 1 - step)

    def table_copy(step):
        return pltpu.make_async_copy(
            table_hbm.at[block_of(step)], table_buf.at[step], table_sem.at[step]
        )

    for step in range(BLOCKS):
        table_copy(step).start()

    barrier = pltpu.get_barrier_semaphore()
    for step in range(1, group_count):
        pl.semaphore_signal(
            barrier, inc=1, device_id={"sta": (me + step) % group_count}, device_id_type=MESH
        )
    pl.semaphore_signal(barrier, inc=1, device_id={"tm": 1 - core}, device_id_type=MESH)

    tail = strain_buf.shape[0] - seg_count * SEG_LEN
    strain_buf[pl.ds(seg_count * SEG_LEN, tail), :] = jnp.zeros((tail, channels), BF16)
    edge = jnp.zeros((BLOCK, channels), BF16)
    for seg in range(seg_count):
        for buf in (high_buf, low_buf):
            buf[seg, pl.ds(0, BLOCK), :] = edge
            buf[seg, pl.ds((BLOCKS + 1) * BLOCK, BLOCK), :] = edge
    numbers = lax.broadcasted_iota(jnp.int32, (channels, CHUNK), 0) + 1
    iota_buf[...] = numbers.astype(F32).astype(BF16)

    owners = owner_ref[...]
    hot = (owners == lax.broadcasted_iota(jnp.int32, (pairs, 128), 1)).astype(F32)
    before = lax.broadcasted_iota(jnp.int32, (pairs, pairs), 0) > lax.broadcasted_iota(
        jnp.int32, (pairs, pairs), 1
    )
    earlier = dot(before.astype(F32).astype(BF16), hot.astype(BF16))
    slot = jnp.sum(earlier * hot, axis=1, keepdims=True).astype(jnp.int32)
    target = owners * capacity + slot
    placed = (target == lax.broadcasted_iota(jnp.int32, (pairs, slots), 1)).astype(F32).astype(BF16)
    kind = lax.broadcasted_iota(jnp.int32, (8, pairs), 0) % 4
    turn = lax.broadcasted_iota(jnp.int32, (8, pairs), 1) // pair_count
    near = jnp.concatenate([local_ref[pl.ds(r, 1), :] for r in range(round_count)], axis=1) + 1
    far = jnp.concatenate([remote_ref[pl.ds(r, 1), :] for r in range(round_count)], axis=1) + 1
    listed = jnp.where(kind == 0, near, jnp.where(kind == turn + 1, far, 0))
    ordered = dot(listed.astype(F32).astype(BF16), placed)
    first = lax.broadcasted_iota(jnp.int32, (8, CHUNK), 0) < 4
    tiles = []
    for chunk in range(0, chunks, 2):
        even = ordered[:, chunk * CHUNK : (chunk + 1) * CHUNK]
        odd = ordered[:, (chunk + 1) * CHUNK : (chunk + 2) * CHUNK]
        tiles.append(jnp.where(first, even, odd))
    own_index = jnp.concatenate(tiles, axis=0).astype(BF16)
    index_out[...] = own_index
    index_buf[me] = own_index
    pl.semaphore_wait(barrier, group_count)

    def index_copy(step):
        there = (me + step) % group_count
        return pltpu.make_async_remote_copy(
            src_ref=index_out,
            dst_ref=index_buf.at[me],
            send_sem=isend_sem.at[step - 1],
            recv_sem=irecv_sem.at[step - 1],
            device_id={"sta": there},
            device_id_type=MESH,
        )

    for step in range(1, group_count):
        index_copy(step).start()

    band_row = lax.broadcasted_iota(jnp.int32, (BLOCK, 3 * BLOCK), 0) + BLOCK
    band_col = lax.broadcasted_iota(jnp.int32, (BLOCK, 3 * BLOCK), 1)
    band = (jnp.abs(band_row - band_col) <= WIN).astype(F32).astype(BF16)

    def transform(step):
        table_copy(step).wait()
        for seg in range(seg_count):
            spectra = dot(table_buf[step], strain_buf[pl.ds(seg * SEG_LEN, SEG_PAD), :])
            spec_buf[step % 2, seg] = spectra
            real, imag = spectra[:BLOCK], spectra[BLOCK:]
            amplitude = jnp.sqrt(real * real + imag * imag)
            high = amplitude.astype(BF16)
            place = pl.ds(pl.multiple_of((block_of(step) + 1) * BLOCK, BLOCK), BLOCK)
            high_buf[seg, place, :] = high
            low_buf[seg, place, :] = (amplitude - high.astype(F32)).astype(BF16)

    def bulk_copy(number, source):
        return pltpu.make_async_remote_copy(
            src_ref=sent_buf.at[number],
            dst_ref=got_buf.at[source],
            send_sem=send_sem.at[number],
            recv_sem=recv_sem.at[source],
            device_id={"sta": number},
            device_id_type=MESH,
        )

    def whiten(step):
        block = block_of(step)
        around = pl.ds(pl.multiple_of(block * BLOCK, BLOCK), 3 * BLOCK)
        for seg in range(seg_count):
            total = dot(band, high_buf[seg, around, :]) + dot(band, low_buf[seg, around, :])
            inverse = 1.0 / (total * (1.0 / (2 * WIN + 1)) + EPSILON)
            for part in range(per_block):
                inside = inverse[part * bins : (part + 1) * bins]
                real = spec_buf[step % 2, seg, part * bins : (part + 1) * bins, :] * inside
                imag = spec_buf[step % 2, seg, BLOCK + part * bins : BLOCK + (part + 1) * bins, :]
                both = jnp.concatenate([real, imag * inside], axis=0).astype(BF16)
                sent_buf[block * per_block + part, seg * rows : (seg + 1) * rows, :] = both
        for part in range(per_block):
            number = block * per_block + part

            @pl.when(number != me)
            def _():
                bulk_copy(number, me).start()

            @pl.when(number == me)
            def _():
                got_buf[me] = sent_buf[me]

    strain_copy.wait()
    transform(0)

    def body(step, carry):
        transform(step)
        whiten(step - 1)
        return carry

    lax.fori_loop(1, BLOCKS, body, 0)
    whiten(BLOCKS - 1)

    for step in range(1, group_count):
        index_copy(step).wait_recv()

    def arrived(source, carry):
        @pl.when(source != me)
        def _():
            bulk_copy(source, source).wait_recv()

        return carry

    lax.fori_loop(0, group_count, arrived, 0)

    per_tile = 128 // capacity
    group_tiles = group_count // per_tile
    half_tiles = group_tiles // 2
    lane = lax.broadcasted_iota(jnp.int32, (COEFS, 128), 1) // capacity
    one, zero = jnp.ones((channels, CHUNK), BF16), jnp.zeros((channels, CHUNK), BF16)

    def selection(row):
        return jnp.where(iota_buf[...] == row, one, zero)

    def coefficients(group):
        listed = index_buf[group]
        own = got_buf[group]
        peers = [got_buf[jnp.bitwise_xor(group, masks_ref[r])] for r in range(round_count)]
        result = []
        for chunk in range(chunks):
            row = 4 * chunk
            a = dot(own, selection(listed[row : row + 1]))
            b = dot(peers[0], selection(listed[row + 1 : row + 2]))
            for r in range(1, round_count):
                b = b + dot(peers[r], selection(listed[row + 1 + r : row + 2 + r]))
            real, imag = 0.0, 0.0
            for seg in range(seg_count):
                low = seg * rows
                ar, ai = a[low : low + bins], a[low + bins : low + rows]
                br, bi = b[low : low + bins], b[low + bins : low + rows]
                real = real + (ar * br + ai * bi)
                imag = imag + (ai * br - ar * bi)
            cross = jnp.concatenate([real, imag], axis=0).astype(BF16)
            both = dot(left_ref[...], cross)
            result.append(both[:COEFS] + both[COEFS:])
        return jnp.concatenate(result, axis=1)

    def tile_of(tile):
        parts = [coefficients(tile * per_tile + i) for i in range(per_tile)]
        blocks = []
        for owner_tile in range(slots // 128):
            cut = [p[:, owner_tile * 128 : (owner_tile + 1) * 128] for p in parts]
            for o in range(per_tile):
                block = cut[0] if o == 0 else pltpu.roll(cut[0], (128 - o * capacity) % 128, 1)
                for i in range(1, per_tile):
                    turned = cut[i]
                    if i != o:
                        turned = pltpu.roll(turned, ((i - o) * capacity) % 128, 1)
                    block = jnp.where(lane == i, turned, block)
                blocks.append(block)
        return blocks

    def part_copy(number):
        return pltpu.make_async_remote_copy(
            src_ref=part_buf.at[number],
            dst_ref=sum_in.at[number],
            send_sem=psend_sem.at[number],
            recv_sem=precv_sem.at[number],
            device_id={"tm": 1 - core},
            device_id_type=MESH,
        )

    def theirs(number, carry):
        blocks = tile_of((1 - core) * half_tiles + number)
        for o in range(group_count):
            part_buf[number, o] = blocks[o].astype(BF16)
        part_copy(number).start()
        return carry

    lax.fori_loop(0, half_tiles, theirs, 0)

    for number in range(half_tiles):
        blocks = tile_of(core * half_tiles + number)
        part_copy(number).wait_recv()
        for o in range(group_count):
            total = blocks[o] + sum_in[number, o].astype(F32)
            res_buf[o, :, number * 128 : (number + 1) * 128] = total.astype(BF16)

    width = half_tiles * 128

    def slot_of(source, side):
        return out_ref.at[
            pl.ds(pl.multiple_of(source * COEFS, COEFS), COEFS),
            pl.ds(pl.multiple_of(side * width, width), width),
        ]

    def result_copy(number, source):
        return pltpu.make_async_remote_copy(
            src_ref=res_buf.at[number],
            dst_ref=slot_of(source, core),
            send_sem=rsend_sem.at[number],
            recv_sem=rrecv_sem.at[source],
            device_id={"sta": number},
            device_id_type=MESH,
        )

    def forward_copy(source, side):
        return pltpu.make_async_remote_copy(
            src_ref=slot_of(source, side),
            dst_ref=slot_of(source, side),
            send_sem=fsend_sem.at[source],
            recv_sem=frecv_sem.at[source],
            device_id={"tm": 1 - core},
            device_id_type=MESH,
        )

    for step in range(1, group_count):
        there = (me + step + group_count // 2) % group_count

        @pl.when(there != me)
        def _():
            result_copy(there, me).start()

    there = (me + group_count // 2) % group_count
    result_copy(there, me).start()
    own_copy = pltpu.make_async_copy(res_buf.at[me], slot_of(me, core), own_sem)
    own_copy.start()
    own_copy.wait()
    forward_copy(me, core).start()
    for step in range(1, group_count):
        source = (me + step) % group_count
        result_copy(source, source).wait_recv()
        forward_copy(source, core).start()
    for source in range(group_count):
        forward_copy(source, 1 - core).wait_recv()
        forward_copy(source, core).wait_send()
    for step in range(1, group_count):
        there = (me + step) % group_count
        result_copy(there, me).wait_send()
        bulk_copy(there, me).wait_send()
        index_copy(step).wait_send()
    for number in range(half_tiles):
        part_copy(number).wait_send()


def per_device(strain, masks, pair_local, pair_remote, owner):
    group_count = lax.axis_size("sta")
    time_count = lax.axis_size("tm")
    seg_count = strain.shape[0] // SEG_LEN
    channels = strain.shape[1]
    round_count, pair_count = pair_local.shape
    capacity = max(2, 2 * round_count * pair_count // group_count)
    slots = group_count * capacity
    bins = FREQS // group_count
    rows = seg_count * 2 * bins
    norm_scale = 1.0 / math.sqrt(seg_count * time_count * FREQS)
    left, right = inverse_factors(group_count, norm_scale)
    left = lax.dynamic_index_in_dim(jnp.asarray(left), lax.axis_index("sta"), 0, keepdims=False)
    half_tiles = slots // 256
    dma = pltpu.SemaphoreType.DMA
    vmem = pl.BlockSpec(memory_space=pltpu.VMEM)
    coefs = pl.pallas_call(
        functools.partial(main_kernel, group_count, capacity, seg_count, pair_local.shape),
        out_shape=jax.ShapeDtypeStruct((group_count * COEFS, slots), BF16),
        in_specs=[pl.BlockSpec(memory_space=pl.ANY)] * 2
        + [vmem] * 4
        + [pl.BlockSpec(memory_space=pltpu.SMEM)],
        out_specs=vmem,
        scratch_shapes=[
            pltpu.VMEM(((seg_count - 1) * SEG_LEN + SEG_PAD, channels), BF16),
            pltpu.VMEM((BLOCKS, 2 * BLOCK, SEG_PAD), BF16),
            pltpu.VMEM((2, seg_count, 2 * BLOCK, channels), F32),
            pltpu.VMEM((seg_count, (BLOCKS + 2) * BLOCK, channels), BF16),
            pltpu.VMEM((seg_count, (BLOCKS + 2) * BLOCK, channels), BF16),
            pltpu.VMEM((channels, CHUNK), BF16),
            pltpu.VMEM((group_count, rows, channels), BF16),
            pltpu.VMEM((group_count, rows, channels), BF16),
            pltpu.VMEM((16, CHUNK), BF16),
            pltpu.VMEM((group_count, 16, CHUNK), BF16),
            pltpu.VMEM((half_tiles, group_count, COEFS, 128), BF16),
            pltpu.VMEM((half_tiles, group_count, COEFS, 128), BF16),
            pltpu.VMEM((group_count, COEFS, half_tiles * 128), BF16),
            dma(()),
            dma((BLOCKS,)),
            dma((group_count,)),
            dma((group_count,)),
            dma((group_count - 1,)),
            dma((group_count - 1,)),
            dma((half_tiles,)),
            dma((half_tiles,)),
            dma((group_count,)),
            dma((group_count,)),
            dma((group_count,)),
            dma((group_count,)),
            dma(()),
        ],
        compiler_params=pltpu.CompilerParams(
            collective_id=0, has_side_effects=True, vmem_limit_bytes=48 * 1024 * 1024
        ),
    )(strain, jnp.asarray(forward_blocks()), left, pair_local, pair_remote, owner, masks)
    width = LAGS // time_count
    mine = lax.dynamic_slice_in_dim(
        jnp.asarray(right), lax.axis_index("tm") * width, width, axis=1
    )
    return jnp.einsum("cs,cl->sl", coefs, mine, preferred_element_type=F32)


def solution(mesh):
    placed = (P("tm", "sta"), P(), P(None, "sta"), P(None, "sta"), P("sta", None))
    return jax.shard_map(
        per_device, mesh=mesh, in_specs=placed, out_specs=P("sta", "tm"), check_vma=False
    )
```

```python
import functools
import math

import jax
import jax.numpy as jnp
import ml_dtypes
import numpy as np
from jax import lax
from jax.experimental import pallas as pl
from jax.experimental.pallas import tpu as pltpu
from jax.sharding import PartitionSpec as P

SEG_LEN = 6000
SEG_PAD = 6144
FREQS = 512
WIN = 32
LAGS = 512
EPSILON = 1e-06
BLOCK = 64
BLOCKS = FREQS // BLOCK
CHUNK = 256
COEFS = 16
LEFT_ROW = SEG_PAD // 128
F32 = jnp.float32
BF16 = jnp.bfloat16
MESH = pl.DeviceIdType.MESH


def angles_of(product):
    return np.mod(product, SEG_LEN).astype(np.float32) * np.float32(2.0 * math.pi / SEG_LEN)


def forward_blocks():
    angles = angles_of(np.arange(1, FREQS + 1)[:, None] * np.arange(SEG_LEN)[None, :])
    table = np.zeros((BLOCKS, 2, BLOCK, SEG_PAD), np.float32)
    table[:, 0, :, :SEG_LEN] = np.cos(angles).reshape(BLOCKS, BLOCK, SEG_LEN)
    table[:, 1, :, :SEG_LEN] = -np.sin(angles).reshape(BLOCKS, BLOCK, SEG_LEN)
    return table.reshape(BLOCKS, 2 * BLOCK, SEG_PAD).astype(ml_dtypes.bfloat16)


def inverse_factors(slices, scale):
    angles = angles_of(np.arange(1, FREQS + 1)[:, None] * (np.arange(LAGS) - LAGS // 2)[None, :])
    angles = angles.astype(np.float64)
    bins = FREQS // slices
    left, right = [], []
    for number in range(slices):
        part = angles[number * bins : (number + 1) * bins]
        u, s, vt = np.linalg.svd(np.concatenate([np.cos(part), -np.sin(part)]), full_matrices=False)
        left.append(u[:, :COEFS].T)
        right.append(s[:COEFS, None] * vt[:COEFS] * scale)
    left = np.stack(left).astype(np.float32)
    high = left.astype(ml_dtypes.bfloat16)
    low = (left - high.astype(np.float32)).astype(ml_dtypes.bfloat16)
    return np.concatenate([high, low], axis=1), np.concatenate(right).astype(ml_dtypes.bfloat16)


def tables(left):
    last = np.zeros((2 * BLOCK, SEG_PAD), ml_dtypes.bfloat16)
    for number, block in enumerate(left):
        row, col = number // LEFT_ROW * 2 * COEFS, number % LEFT_ROW * 128
        last[row : row + 2 * COEFS, col : col + block.shape[1]] = block
    return np.concatenate([forward_blocks(), last[None]])


def dot(left, right):
    return jnp.dot(left, right, preferred_element_type=F32)


def main_kernel(
    group_count, capacity, seg_count, pair_shape,
    strain_hbm, table_hbm, lists_ref,
    out_ref,
    strain_buf, table_buf, left_ref, masks_ref,
    spec_buf, high_buf, low_buf, iota_buf, sent_buf, got_buf,
    near_buf, full_buf, other_buf,
    index_out, index_buf, part_buf, sum_in, res_buf,
    small_sem, strain_sem, table_sem, send_sem, recv_sem, isend_sem, irecv_sem,
    psend_sem, precv_sem, rsend_sem, rrecv_sem, fsend_sem, frecv_sem, own_sem,
):
    round_count, pair_count = pair_shape
    pairs = round_count * pair_count
    bins = FREQS // group_count
    per_block = BLOCK // bins
    rows = 2 * bins
    slots = group_count * capacity
    chunks = slots // CHUNK
    channels = strain_hbm.shape[1]
    half, quarter = group_count // 2, group_count // 4
    full_mask = group_count - 1
    me, core = lax.axis_index("sta"), lax.axis_index("tm")
    upper = me >= half
    near_base = jnp.where(upper, half, 0)
    far_base = half - near_base

    mask_row = 1 + 2 * round_count
    masks_copy = pltpu.make_async_copy(lists_ref.at[pl.ds(mask_row, 1)], masks_ref, small_sem.at[0])
    masks_copy.start()
    left_copy = pltpu.make_async_copy(
        table_hbm.at[
            BLOCKS,
            pl.ds(pl.multiple_of(me // LEFT_ROW * 2 * COEFS, 2 * COEFS), 2 * COEFS),
            pl.ds(pl.multiple_of(me % LEFT_ROW * 128, 128), 128),
        ],
        left_ref,
        small_sem.at[1],
    )
    left_copy.start()
    strain_copy = pltpu.make_async_copy(
        strain_hbm, strain_buf.at[pl.ds(0, seg_count * SEG_LEN)], strain_sem
    )
    strain_copy.start()

    def block_of(step):
        return jnp.where(upper, step, BLOCKS - 1 - step)

    def table_copy(step):
        return pltpu.make_async_copy(
            table_hbm.at[block_of(step)], table_buf.at[step], table_sem.at[step]
        )

    for step in range(2):
        table_copy(step).start()

    barrier = pltpu.get_barrier_semaphore()
    for step in range(1, group_count):
        pl.semaphore_signal(
            barrier, inc=1, device_id={"sta": (me + step) % group_count}, device_id_type=MESH
        )
    pl.semaphore_signal(barrier, inc=1, device_id={"tm": 1 - core}, device_id_type=MESH)

    tail = strain_buf.shape[0] - seg_count * SEG_LEN
    strain_buf[pl.ds(seg_count * SEG_LEN, tail), :] = jnp.zeros((tail, channels), BF16)
    edge = jnp.zeros((BLOCK, channels), BF16)
    for seg in range(seg_count):
        for buf in (high_buf, low_buf):
            buf[seg, pl.ds(0, BLOCK), :] = edge
            buf[seg, pl.ds((BLOCKS + 1) * BLOCK, BLOCK), :] = edge
    numbers = lax.broadcasted_iota(jnp.int32, (channels, CHUNK), 0) + 1
    iota_buf[...] = numbers.astype(F32).astype(BF16)

    masks_copy.wait()
    left_copy.wait()

    def one_row(first):
        return jnp.concatenate(
            [lists_ref[first + r : first + r + 1, :pair_count] for r in range(round_count)], axis=1
        )

    owners = lists_ref[0:1, :]
    hot = (owners == lax.broadcasted_iota(jnp.int32, (group_count, pairs), 0)).astype(F32)
    before = lax.broadcasted_iota(jnp.int32, (pairs, pairs), 0) < lax.broadcasted_iota(
        jnp.int32, (pairs, pairs), 1
    )
    earlier = dot(hot.astype(BF16), before.astype(F32).astype(BF16))
    slot = jnp.sum(earlier * hot, axis=0, keepdims=True).astype(jnp.int32)
    target = owners * capacity + slot
    placed = (target == lax.broadcasted_iota(jnp.int32, (slots, pairs), 0)).astype(F32).astype(BF16)
    kind = lax.broadcasted_iota(jnp.int32, (8, pairs), 0) % 4
    turn = lax.broadcasted_iota(jnp.int32, (8, pairs), 1) // pair_count
    first_kind = jnp.where(masks_ref[0, 0] == full_mask, 1, 2)
    far_kind = jnp.where(turn == 0, first_kind, 3 - first_kind)
    near, far = one_row(1) + 1, one_row(1 + round_count) + 1
    listed = jnp.where(kind == 0, near, jnp.where(kind == far_kind, far, 0))
    ordered = lax.dot_general(
        listed.astype(F32).astype(BF16),
        placed,
        (((1,), (1,)), ((), ())),
        preferred_element_type=F32,
    )
    first = lax.broadcasted_iota(jnp.int32, (8, CHUNK), 0) < 4
    tiles = []
    for chunk in range(0, chunks, 2):
        even = ordered[:, chunk * CHUNK : (chunk + 1) * CHUNK]
        odd = ordered[:, (chunk + 1) * CHUNK : (chunk + 2) * CHUNK]
        tiles.append(jnp.where(first, even, odd))
    own_index = jnp.concatenate(tiles, axis=0).astype(BF16)
    index_out[...] = own_index
    index_buf[me] = own_index
    pl.semaphore_wait(barrier, group_count)

    def index_copy(step):
        there = (me + step) % group_count
        return pltpu.make_async_remote_copy(
            src_ref=index_out,
            dst_ref=index_buf.at[me],
            send_sem=isend_sem.at[step - 1],
            recv_sem=irecv_sem.at[step - 1],
            device_id={"sta": there},
            device_id_type=MESH,
        )

    for step in range(1, group_count):
        index_copy(step).start()

    band_row = lax.broadcasted_iota(jnp.int32, (BLOCK, 3 * BLOCK), 0) + BLOCK
    band_col = lax.broadcasted_iota(jnp.int32, (BLOCK, 3 * BLOCK), 1)
    band = (jnp.abs(band_row - band_col) <= WIN).astype(F32).astype(BF16)

    def transform(step):
        table_copy(step).wait()

        @pl.when(step + 2 < BLOCKS)
        def _():
            table_copy(step + 2).start()

        for seg in range(seg_count):
            spectra = dot(table_buf[step], strain_buf[pl.ds(seg * SEG_LEN, SEG_PAD), :])
            spec_buf[step % 2, seg] = spectra
            real, imag = spectra[:BLOCK], spectra[BLOCK:]
            amplitude = jnp.sqrt(real * real + imag * imag)
            high = amplitude.astype(BF16)
            place = pl.ds(pl.multiple_of((block_of(step) + 1) * BLOCK, BLOCK), BLOCK)
            high_buf[seg, place, :] = high
            low_buf[seg, place, :] = (amplitude - high.astype(F32)).astype(BF16)

    def bulk_copy(number, source):
        return pltpu.make_async_remote_copy(
            src_ref=sent_buf.at[number],
            dst_ref=got_buf.at[source],
            send_sem=send_sem.at[number],
            recv_sem=recv_sem.at[source],
            device_id={"sta": number},
            device_id_type=MESH,
        )

    def whiten(step):
        block = block_of(step)
        around = pl.ds(pl.multiple_of(block * BLOCK, BLOCK), 3 * BLOCK)
        for seg in range(seg_count):
            total = dot(band, high_buf[seg, around, :]) + dot(band, low_buf[seg, around, :])
            inverse = 1.0 / (total * (1.0 / (2 * WIN + 1)) + EPSILON)
            for part in range(per_block):
                inside = inverse[part * bins : (part + 1) * bins]
                real = spec_buf[step % 2, seg, part * bins : (part + 1) * bins, :] * inside
                imag = spec_buf[step % 2, seg, BLOCK + part * bins : BLOCK + (part + 1) * bins, :]
                both = jnp.concatenate([real, imag * inside], axis=0).astype(BF16)
                sent_buf[block * per_block + part, seg * rows : (seg + 1) * rows, :] = both

        @pl.when(step < 2)
        def _():
            for part in range(per_block):
                bulk_copy(block * per_block + part, me).start()

        @pl.when(step == 3)
        def _():
            base = jnp.where(upper, quarter, half)
            for part in range(quarter):
                bulk_copy(base + (me + part) % quarter, me).start()

        @pl.when(step >= 4)
        def _():
            for part in range(per_block):
                number = block * per_block + part

                @pl.when(number != me)
                def _():
                    bulk_copy(number, me).start()

                @pl.when(number == me)
                def _():
                    got_buf[me] = sent_buf[me]

    strain_copy.wait()
    transform(0)

    def body(step, carry):
        transform(step)
        whiten(step - 1)
        return carry

    lax.fori_loop(1, BLOCKS, body, 0)
    whiten(BLOCKS - 1)

    for step in range(1, group_count):
        index_copy(step).wait_recv()

    one, zero = jnp.ones((channels, CHUNK), BF16), jnp.zeros((channels, CHUNK), BF16)
    other_mask = masks_ref[0, 0] ^ masks_ref[0, 1] ^ full_mask
    other_mask = jnp.bitwise_and(other_mask, full_mask)

    def pick(source):
        block = got_buf[source]
        partner = full_mask - source
        listed = [
            index_buf[source],
            index_buf[partner],
            index_buf[jnp.bitwise_xor(source, other_mask)],
        ]
        places = [near_buf.at[source], full_buf.at[partner], other_buf.at[source]]
        for chunk in range(chunks):
            for n in range(3):
                row = listed[n][4 * chunk + n : 4 * chunk + n + 1]
                chosen = dot(block, jnp.where(iota_buf[...] == row, one, zero))
                places[n][:, chunk * CHUNK : (chunk + 1) * CHUNK] = chosen.astype(BF16)

    def near_group(number, carry):
        source = near_base + (me + number) % half

        @pl.when(source != me)
        def _():
            bulk_copy(source, source).wait_recv()

        pick(source)
        return carry

    def far_group(number, carry):
        source = far_base + (me - number // 2 + group_count) % quarter + quarter * (number % 2)
        bulk_copy(source, source).wait_recv()
        pick(source)
        return carry

    lax.fori_loop(0, half, near_group, 0)
    lax.fori_loop(0, half, far_group, 0)

    per_tile = 128 // capacity
    group_tiles = group_count // per_tile
    half_tiles = group_tiles // 2
    lane = lax.broadcasted_iota(jnp.int32, (COEFS, 128), 1) // capacity

    def coefficients(group):
        peer = jnp.bitwise_xor(group, other_mask)
        result = []
        for chunk in range(chunks):
            lanes = slice(chunk * CHUNK, (chunk + 1) * CHUNK)
            real, imag = 0.0, 0.0
            for seg in range(seg_count):
                low = seg * rows
                a = near_buf[group, low : low + rows, lanes].astype(F32)
                b = full_buf[group, low : low + rows, lanes]
                b = (b + other_buf[peer, low : low + rows, lanes]).astype(F32)
                ar, ai, br, bi = a[:bins], a[bins:], b[:bins], b[bins:]
                real = real + (ar * br + ai * bi)
                imag = imag + (ai * br - ar * bi)
            cross = jnp.concatenate([real, imag], axis=0).astype(BF16)
            both = dot(left_ref[:, :rows], cross)
            result.append(both[:COEFS] + both[COEFS:])
        return jnp.concatenate(result, axis=1)

    def tile_of(tile):
        parts = [coefficients(tile * per_tile + i) for i in range(per_tile)]
        blocks = []
        for owner_tile in range(slots // 128):
            cut = [p[:, owner_tile * 128 : (owner_tile + 1) * 128] for p in parts]
            for o in range(per_tile):
                block = cut[0] if o == 0 else pltpu.roll(cut[0], (128 - o * capacity) % 128, 1)
                for i in range(1, per_tile):
                    turned = cut[i]
                    if i != o:
                        turned = pltpu.roll(turned, ((i - o) * capacity) % 128, 1)
                    block = jnp.where(lane == i, turned, block)
                blocks.append(block)
        return blocks

    def part_copy(number):
        return pltpu.make_async_remote_copy(
            src_ref=part_buf.at[number],
            dst_ref=sum_in.at[number],
            send_sem=psend_sem.at[number],
            recv_sem=precv_sem.at[number],
            device_id={"tm": 1 - core},
            device_id_type=MESH,
        )

    def slot_of(source, side, stage):
        start = (2 * side + stage) * stage_width
        return out_ref.at[
            pl.ds(pl.multiple_of(source * COEFS, COEFS), COEFS),
            pl.ds(pl.multiple_of(start, stage_width), stage_width),
        ]

    stage_tiles = half_tiles // 2
    stage_width = stage_tiles * 128

    def result_copy(number, source, stage):
        return pltpu.make_async_remote_copy(
            src_ref=res_buf.at[stage, number],
            dst_ref=slot_of(source, core, stage),
            send_sem=rsend_sem.at[stage, number],
            recv_sem=rrecv_sem.at[stage, source],
            device_id={"sta": number},
            device_id_type=MESH,
        )

    def forward_copy(source, side, stage):
        return pltpu.make_async_remote_copy(
            src_ref=slot_of(source, side, stage),
            dst_ref=slot_of(source, side, stage),
            send_sem=fsend_sem.at[stage, source],
            recv_sem=frecv_sem.at[stage, source],
            device_id={"tm": 1 - core},
            device_id_type=MESH,
        )

    def own_copy(stage):
        return pltpu.make_async_copy(
            res_buf.at[stage, me], slot_of(me, core, stage), own_sem.at[stage]
        )

    def stage_of(stage, carry):
        def theirs(number, carry):
            blocks = tile_of((1 - core) * half_tiles + number)
            for o in range(group_count):
                part_buf[number, o] = blocks[o].astype(BF16)
            part_copy(number).start()
            return carry

        lax.fori_loop(stage * stage_tiles, (stage + 1) * stage_tiles, theirs, 0)
        for n in range(stage_tiles):
            number = stage * stage_tiles + n
            blocks = tile_of(core * half_tiles + number)
            part_copy(number).wait_recv()
            for o in range(group_count):
                total = blocks[o] + sum_in[number, o].astype(F32)
                res_buf[stage, o, :, n * 128 : (n + 1) * 128] = total.astype(BF16)
        for step in range(group_count):
            there = (me + step + half) % group_count
            if step == half:
                own_copy(stage).start()
            else:
                result_copy(there, me, stage).start()
        return carry

    lax.fori_loop(0, 2, stage_of, 0)

    for stage in range(2):
        own_copy(stage).wait()
        forward_copy(me, core, stage).start()
        for step in range(1, group_count):
            source = (me + step) % group_count
            result_copy(source, source, stage).wait_recv()
            forward_copy(source, core, stage).start()
    for stage in range(2):
        for source in range(group_count):
            forward_copy(source, 1 - core, stage).wait_recv()
            forward_copy(source, core, stage).wait_send()
        for step in range(1, group_count):
            result_copy((me + step) % group_count, me, stage).wait_send()
    for step in range(1, group_count):
        bulk_copy((me + step) % group_count, me).wait_send()
        index_copy(step).wait_send()
    for number in range(half_tiles):
        part_copy(number).wait_send()


def per_device(strain, masks, pair_local, pair_remote, owner):
    group_count = lax.axis_size("sta")
    time_count = lax.axis_size("tm")
    seg_count = strain.shape[0] // SEG_LEN
    channels = strain.shape[1]
    round_count, pair_count = pair_local.shape
    capacity = max(2, 2 * round_count * pair_count // group_count)
    slots = group_count * capacity
    bins = FREQS // group_count
    rows = seg_count * 2 * bins
    norm_scale = 1.0 / math.sqrt(seg_count * time_count * FREQS)
    left, right = inverse_factors(group_count, norm_scale)
    half_tiles = slots // 256
    pairs = round_count * pair_count
    lists = owner.reshape(1, pairs)
    for array in (pair_local, pair_remote, masks[None, :]):
        array = jnp.pad(array, ((0, 0), (0, pairs - array.shape[1])))
        lists = jnp.concatenate([lists, array])
    dma = pltpu.SemaphoreType.DMA
    vmem = pl.BlockSpec(memory_space=pltpu.VMEM)
    coefs = pl.pallas_call(
        functools.partial(main_kernel, group_count, capacity, seg_count, pair_local.shape),
        out_shape=jax.ShapeDtypeStruct((group_count * COEFS, slots), BF16),
        in_specs=[pl.BlockSpec(memory_space=pl.ANY)] * 2 + [vmem],
        out_specs=vmem,
        scratch_shapes=[
            pltpu.VMEM(((seg_count - 1) * SEG_LEN + SEG_PAD, channels), BF16),
            pltpu.VMEM((BLOCKS, 2 * BLOCK, SEG_PAD), BF16),
            pltpu.VMEM((2 * COEFS, 128), BF16),
            pltpu.SMEM((1, round_count * pair_count), jnp.int32),
            pltpu.VMEM((2, seg_count, 2 * BLOCK, channels), F32),
            pltpu.VMEM((seg_count, (BLOCKS + 2) * BLOCK, channels), BF16),
            pltpu.VMEM((seg_count, (BLOCKS + 2) * BLOCK, channels), BF16),
            pltpu.VMEM((channels, CHUNK), BF16),
            pltpu.VMEM((group_count, rows, channels), BF16),
            pltpu.VMEM((group_count, rows, channels), BF16),
            pltpu.VMEM((group_count, rows, slots), BF16),
            pltpu.VMEM((group_count, rows, slots), BF16),
            pltpu.VMEM((group_count, rows, slots), BF16),
            pltpu.VMEM((16, CHUNK), BF16),
            pltpu.VMEM((group_count, 16, CHUNK), BF16),
            pltpu.VMEM((half_tiles, group_count, COEFS, 128), BF16),
            pltpu.VMEM((half_tiles, group_count, COEFS, 128), BF16),
            pltpu.VMEM((2, group_count, COEFS, half_tiles * 64), BF16),
            dma((2,)),
            dma(()),
            dma((BLOCKS,)),
            dma((group_count,)),
            dma((group_count,)),
            dma((group_count - 1,)),
            dma((group_count - 1,)),
            dma((half_tiles,)),
            dma((half_tiles,)),
            dma((2, group_count)),
            dma((2, group_count)),
            dma((2, group_count)),
            dma((2, group_count)),
            dma((2,)),
        ],
        compiler_params=pltpu.CompilerParams(
            collective_id=0, has_side_effects=True, vmem_limit_bytes=48 * 1024 * 1024
        ),
    )(strain, jnp.asarray(tables(left)), lists)
    width = LAGS // time_count
    mine = lax.dynamic_slice_in_dim(
        jnp.asarray(right), lax.axis_index("tm") * width, width, axis=1
    )
    return jnp.einsum("cs,cl->sl", coefs, mine, preferred_element_type=F32)


def solution(mesh):
    placed = (P("tm", "sta"), P(), P(None, "sta"), P(None, "sta"), P("sta", None))
    return jax.shard_map(
        per_device, mesh=mesh, in_specs=placed, out_specs=P("sta", "tm"), check_vma=False
    )
```

```python
import functools
import math

import jax
import jax.numpy as jnp
import ml_dtypes
import numpy as np
from jax import lax
from jax.experimental import pallas as pl
from jax.experimental.pallas import tpu as pltpu
from jax.sharding import PartitionSpec as P

SEG_LEN = 6000
SEG_PAD = 6144
FREQS = 512
WIN = 32
LAGS = 512
EPSILON = 1e-06
BLOCK = 64
BLOCKS = FREQS // BLOCK
CHUNK = 256
COEFS = 16
STAGES = 2
LEFT_ROW = SEG_PAD // 128
F32 = jnp.float32
BF16 = jnp.bfloat16
MESH = pl.DeviceIdType.MESH


def angles_of(product):
    return np.mod(product, SEG_LEN).astype(np.float32) * np.float32(2.0 * math.pi / SEG_LEN)


def forward_blocks():
    angles = angles_of(np.arange(1, FREQS + 1)[:, None] * np.arange(SEG_LEN)[None, :])
    table = np.zeros((BLOCKS, 2, BLOCK, SEG_PAD), np.float32)
    table[:, 0, :, :SEG_LEN] = np.cos(angles).reshape(BLOCKS, BLOCK, SEG_LEN)
    table[:, 1, :, :SEG_LEN] = -np.sin(angles).reshape(BLOCKS, BLOCK, SEG_LEN)
    return table.reshape(BLOCKS, 2 * BLOCK, SEG_PAD).astype(ml_dtypes.bfloat16)


def inverse_factors(slices, scale):
    angles = angles_of(np.arange(1, FREQS + 1)[:, None] * (np.arange(LAGS) - LAGS // 2)[None, :])
    angles = angles.astype(np.float64)
    bins = FREQS // slices
    left, right = [], []
    for number in range(slices):
        part = angles[number * bins : (number + 1) * bins]
        u, s, vt = np.linalg.svd(np.concatenate([np.cos(part), -np.sin(part)]), full_matrices=False)
        left.append(u[:, :COEFS].T)
        right.append(s[:COEFS, None] * vt[:COEFS] * scale)
    left = np.stack(left).astype(np.float32)
    high = left.astype(ml_dtypes.bfloat16)
    low = (left - high.astype(np.float32)).astype(ml_dtypes.bfloat16)
    return np.concatenate([high, low], axis=1), np.concatenate(right).astype(ml_dtypes.bfloat16)


def tables(left):
    last = np.zeros((2 * BLOCK, SEG_PAD), ml_dtypes.bfloat16)
    for number, block in enumerate(left):
        row, col = number // LEFT_ROW * 2 * COEFS, number % LEFT_ROW * 128
        last[row : row + 2 * COEFS, col : col + block.shape[1]] = block
    return np.concatenate([forward_blocks(), last[None]])


def home_of(number, group_count):
    half, quarter = group_count // 2, group_count // 4
    odd = number % 2
    return number // half * half + odd * quarter + ((number % half // 2) ^ (odd * (quarter - 1)))


def slice_of(group, group_count):
    half, quarter = group_count // 2, group_count // 4
    odd = group // quarter % 2
    return group // half * half + 2 * ((group % quarter) ^ (odd * (quarter - 1))) + odd


def dot(left, right):
    return jnp.dot(left, right, preferred_element_type=F32)


def main_kernel(
    group_count, capacity, seg_count, pair_shape,
    strain_hbm, table_hbm, lists_ref,
    out_ref,
    strain_buf, table_buf, left_ref, masks_ref, wide_ref,
    spec_buf, high_buf, low_buf, iota_buf, sent_buf, got_buf,
    near_buf, full_buf, other_buf,
    index_out, index_buf, part_buf, sum_in, res_buf,
    small_sem, strain_sem, table_sem, send_sem, recv_sem, isend_sem, irecv_sem,
    psend_sem, precv_sem, rsend_sem, rrecv_sem, fsend_sem, frecv_sem, own_sem,
):
    round_count, pair_count = pair_shape
    pairs = round_count * pair_count
    bins = FREQS // group_count
    per_block = BLOCK // bins
    rows = 2 * bins
    slots = group_count * capacity
    chunks = slots // CHUNK
    channels = strain_hbm.shape[1]
    half, quarter = group_count // 2, group_count // 4
    full_mask = group_count - 1
    me, core = lax.axis_index("sta"), lax.axis_index("tm")
    upper = me >= half
    mine = slice_of(me, group_count)
    near_base = jnp.where(upper, half, 0)
    far_base = half - near_base

    mask_row = 1 + 2 * round_count
    masks_copy = pltpu.make_async_copy(lists_ref.at[pl.ds(mask_row, 1)], masks_ref, small_sem.at[0])
    masks_copy.start()
    left_copy = pltpu.make_async_copy(
        table_hbm.at[
            BLOCKS,
            pl.ds(pl.multiple_of(mine // LEFT_ROW * 2 * COEFS, 2 * COEFS), 2 * COEFS),
            pl.ds(pl.multiple_of(mine % LEFT_ROW * 128, 128), 128),
        ],
        left_ref,
        small_sem.at[1],
    )
    left_copy.start()
    ends = [min(seg * SEG_LEN + SEG_PAD, seg_count * SEG_LEN) for seg in range(seg_count)]
    strain_copies = []
    for seg, (low, high) in enumerate(zip([0] + ends[:-1], ends)):
        place = pl.ds(low, high - low)
        strain_copies.append(
            pltpu.make_async_copy(strain_hbm.at[place], strain_buf.at[place], strain_sem.at[seg])
        )

    def block_of(step):
        return jnp.where(upper, step, BLOCKS - 1 - step)

    def table_copy(step):
        return pltpu.make_async_copy(
            table_hbm.at[block_of(step)], table_buf.at[step], table_sem.at[step]
        )

    strain_copies[0].start()
    table_copy(0).start()
    table_copy(1).start()
    for copy in strain_copies[1:]:
        copy.start()

    barrier = pltpu.get_barrier_semaphore()
    for step in range(1, group_count):
        pl.semaphore_signal(
            barrier, inc=1, device_id={"sta": (me + step) % group_count}, device_id_type=MESH
        )
    pl.semaphore_signal(barrier, inc=1, device_id={"tm": 1 - core}, device_id_type=MESH)

    tail = strain_buf.shape[0] - seg_count * SEG_LEN
    strain_buf[pl.ds(seg_count * SEG_LEN, tail), :] = jnp.zeros((tail, channels), BF16)
    edge = jnp.zeros((BLOCK, channels), BF16)
    for seg in range(seg_count):
        for buf in (high_buf, low_buf):
            buf[seg, pl.ds(0, BLOCK), :] = edge
            buf[seg, pl.ds((BLOCKS + 1) * BLOCK, BLOCK), :] = edge
    numbers = lax.broadcasted_iota(jnp.int32, (channels, CHUNK), 0) + 1
    iota_buf[...] = numbers.astype(F32).astype(BF16)


    def index_copy(step):
        there = (me + step) % group_count
        return pltpu.make_async_remote_copy(
            src_ref=index_out,
            dst_ref=index_buf.at[core, me],
            send_sem=isend_sem.at[step - 1],
            recv_sem=irecv_sem.at[step - 1],
            device_id={"sta": there},
            device_id_type=MESH,
        )

    masks_copy.wait()
    left_copy.wait()

    def one_row(first):
        return jnp.concatenate(
            [lists_ref[first + r : first + r + 1, :pair_count] for r in range(round_count)], axis=1
        )

    owners = lists_ref[0:1, :]
    hot = (owners == lax.broadcasted_iota(jnp.int32, (group_count, pairs), 0)).astype(F32)
    before = lax.broadcasted_iota(jnp.int32, (pairs, pairs), 0) < lax.broadcasted_iota(
        jnp.int32, (pairs, pairs), 1
    )
    earlier = dot(hot.astype(BF16), before.astype(F32).astype(BF16))
    slot = jnp.sum(earlier * hot, axis=0, keepdims=True).astype(jnp.int32)
    target = owners * capacity + slot
    placed = (target == lax.broadcasted_iota(jnp.int32, (slots, pairs), 0)).astype(F32).astype(BF16)
    kind = lax.broadcasted_iota(jnp.int32, (8, pairs), 0) % 4
    turn = lax.broadcasted_iota(jnp.int32, (8, pairs), 1) // pair_count
    first_kind = jnp.where(masks_ref[0, 0] == full_mask, 1, 2)
    far_kind = jnp.where(turn == 0, first_kind, 3 - first_kind)
    near, far = one_row(1) + 1, one_row(1 + round_count) + 1
    listed = jnp.where(kind == 0, near, jnp.where(kind == far_kind, far, 0))
    ordered = lax.dot_general(
        listed.astype(F32).astype(BF16),
        placed,
        (((1,), (1,)), ((), ())),
        preferred_element_type=F32,
    )
    first = lax.broadcasted_iota(jnp.int32, (8, CHUNK), 0) < 4
    tiles = []
    for chunk in range(0, chunks, 2):
        even = ordered[:, chunk * CHUNK : (chunk + 1) * CHUNK]
        odd = ordered[:, (chunk + 1) * CHUNK : (chunk + 2) * CHUNK]
        tiles.append(jnp.where(first, even, odd))
    own_index = jnp.concatenate(tiles, axis=0).astype(BF16)
    own_index = jnp.where(core == 0, own_index[:, :128], own_index[:, 128:])
    index_out[...] = own_index
    index_buf[core, me] = own_index
    def index_share():
        place = index_buf.at[core]
        return pltpu.make_async_remote_copy(
            src_ref=place,
            dst_ref=place,
            send_sem=isend_sem.at[group_count - 1],
            recv_sem=irecv_sem.at[group_count - 1],
            device_id={"tm": 1 - core},
            device_id_type=MESH,
        )

    pl.semaphore_wait(barrier, group_count)
    for step in range(1, group_count):
        index_copy(step).start()

    band_row = lax.broadcasted_iota(jnp.int32, (BLOCK, 3 * BLOCK), 0) + BLOCK
    band_col = lax.broadcasted_iota(jnp.int32, (BLOCK, 3 * BLOCK), 1)
    band = (jnp.abs(band_row - band_col) <= WIN).astype(F32).astype(BF16)

    def transform_segment(step, seg):
        spectra = dot(table_buf[step], strain_buf[pl.ds(seg * SEG_LEN, SEG_PAD), :])
        spec_buf[step % 2, seg] = spectra
        real, imag = spectra[:BLOCK], spectra[BLOCK:]
        amplitude = jnp.sqrt(real * real + imag * imag)
        high = amplitude.astype(BF16)
        place = pl.ds(pl.multiple_of((block_of(step) + 1) * BLOCK, BLOCK), BLOCK)
        high_buf[seg, place, :] = high
        low_buf[seg, place, :] = (amplitude - high.astype(F32)).astype(BF16)

    def transform(step):
        table_copy(step).wait()

        @pl.when(step + 2 < BLOCKS)
        def _():
            table_copy(step + 2).start()

        for seg in range(seg_count):
            transform_segment(step, seg)

    def bulk_copy(number, source):
        return pltpu.make_async_remote_copy(
            src_ref=sent_buf.at[number],
            dst_ref=got_buf.at[source],
            send_sem=send_sem.at[number],
            recv_sem=recv_sem.at[source],
            device_id={"sta": home_of(number, group_count)},
            device_id_type=MESH,
        )

    def whiten_segment(step, seg):
        block = block_of(step)
        around = pl.ds(pl.multiple_of(block * BLOCK, BLOCK), 3 * BLOCK)
        total = dot(band, high_buf[seg, around, :]) + dot(band, low_buf[seg, around, :])
        inverse = 1.0 / (total * (1.0 / (2 * WIN + 1)) + EPSILON)
        for part in range(per_block):
            inside = inverse[part * bins : (part + 1) * bins]
            real = spec_buf[step % 2, seg, part * bins : (part + 1) * bins, :] * inside
            imag = spec_buf[step % 2, seg, BLOCK + part * bins : BLOCK + (part + 1) * bins, :]
            both = jnp.concatenate([real, imag * inside], axis=0).astype(BF16)
            sent_buf[block * per_block + part, seg * rows : (seg + 1) * rows, :] = both

    def piece_copy(number, seg):
        place = pl.ds(seg * rows, rows)
        return pltpu.make_async_remote_copy(
            src_ref=sent_buf.at[number, place],
            dst_ref=got_buf.at[me, place],
            send_sem=send_sem.at[number],
            recv_sem=recv_sem.at[me],
            device_id={"sta": home_of(number, group_count)},
            device_id_type=MESH,
        )

    def whiten(step):
        block = block_of(step)
        for seg in range(seg_count):
            whiten_segment(step, seg)

        @pl.when(step == 1)
        def _():
            for part in range(per_block):
                bulk_copy(block * per_block + part, me).start()

        @pl.when(step == 3)
        def _():
            base = jnp.where(upper, quarter, half)
            for part in range(quarter):
                bulk_copy(base + (me + part) % quarter, me).start()

        @pl.when(step >= 4)
        def _():
            for part in range(per_block):
                number = block * per_block + part

                @pl.when(number != mine)
                def _():
                    bulk_copy(number, me).start()

                @pl.when(number == mine)
                def _():
                    got_buf[me] = sent_buf[mine]

    for step in range(2):
        table_copy(step).wait()
    for seg in range(seg_count):
        strain_copies[seg].wait()
        if seg == 1:
            for step in range(2, 4):
                table_copy(step).start()
        transform_segment(0, seg)
        transform_segment(1, seg)
        whiten_segment(0, seg)
        for part in range(per_block):
            piece_copy(block_of(0) * per_block + part, seg).start()


    def body(step, carry):
        transform(step)
        whiten(step - 1)
        return carry

    lax.fori_loop(2, BLOCKS, body, 0)
    for step in range(1, group_count):
        index_copy(step).wait_recv()
    index_share().start()
    whiten(BLOCKS - 1)
    index_share().wait()

    one, zero = jnp.ones((channels, CHUNK), BF16), jnp.zeros((channels, CHUNK), BF16)
    other_mask = masks_ref[0, 0] ^ masks_ref[0, 1] ^ full_mask
    other_mask = jnp.bitwise_and(other_mask, full_mask)

    def index_of(group):
        return jnp.concatenate([index_buf[0, group], index_buf[1, group]], axis=1)

    def pick(source):
        block = got_buf[source]
        partner = full_mask - source
        listed = [
            index_of(source),
            index_of(partner),
            index_of(jnp.bitwise_xor(source, other_mask)),
        ]
        places = [near_buf.at[source], full_buf.at[partner], other_buf.at[source]]
        for chunk in range(chunks):
            for n in range(3):
                row = listed[n][4 * chunk + n : 4 * chunk + n + 1]
                chosen = dot(block, jnp.where(iota_buf[...] == row, one, zero))
                places[n][:, chunk * CHUNK : (chunk + 1) * CHUNK] = chosen.astype(BF16)

    def near_group(number, carry):
        source = near_base + (me + number) % half

        @pl.when(source != me)
        def _():
            bulk_copy(source, source).wait_recv()

        pick(source)
        return carry

    def far_group(number, carry):
        source = far_base + (mine - number // 2 + group_count) % quarter + quarter * (number % 2)
        bulk_copy(source, source).wait_recv()
        pick(source)
        return carry

    lax.fori_loop(0, half, near_group, 0)
    lax.fori_loop(0, half, far_group, 0)

    def part_of(shape, axis, size, number):
        return (lax.broadcasted_iota(jnp.int32, shape, axis) // size == number).astype(F32)

    per_tile = 128 // capacity
    group_tiles = group_count // per_tile
    half_tiles = group_tiles // 2
    lane = lax.broadcasted_iota(jnp.int32, (COEFS, 128), 1) // capacity
    tall = jnp.concatenate([left_ref[...].astype(F32)] * per_tile, axis=0)
    widest = sum(
        pltpu.roll(tall, rows * i, 1) * (part_of(tall.shape, 0, 2 * COEFS, i)) for i in range(per_tile)
    )
    wide_ref[...] = widest[:, : rows * per_tile].astype(BF16)

    def cross_of(group, lanes):
        peer = jnp.bitwise_xor(group, other_mask)
        real, imag = 0.0, 0.0
        for seg in range(seg_count):
            low = seg * rows
            a = near_buf[group, low : low + rows, lanes].astype(F32)
            b = full_buf[group, low : low + rows, lanes]
            b = (b + other_buf[peer, low : low + rows, lanes]).astype(F32)
            ar, ai, br, bi = a[:bins], a[bins:], b[:bins], b[bins:]
            real = real + (ar * br + ai * bi)
            imag = imag + (ai * br - ar * bi)
        return jnp.concatenate([real, imag], axis=0).astype(BF16)

    def tile_of(tile):
        found = [[] for _ in range(per_tile)]
        for chunk in range(chunks):
            lanes = slice(chunk * CHUNK, (chunk + 1) * CHUNK)
            cross = [cross_of(tile * per_tile + i, lanes) for i in range(per_tile)]
            both = dot(wide_ref[...], jnp.concatenate(cross, axis=0))
            for i in range(per_tile):
                part = both[2 * COEFS * i : 2 * COEFS * (i + 1)]
                found[i].append(part[:COEFS] + part[COEFS:])
        parts = [jnp.concatenate(f, axis=1) for f in found]
        blocks = []
        for owner_tile in range(slots // 128):
            cut = [p[:, owner_tile * 128 : (owner_tile + 1) * 128] for p in parts]
            for o in range(per_tile):
                block = cut[0] if o == 0 else pltpu.roll(cut[0], (128 - o * capacity) % 128, 1)
                for i in range(1, per_tile):
                    turned = cut[i]
                    if i != o:
                        turned = pltpu.roll(turned, ((i - o) * capacity) % 128, 1)
                    block = jnp.where(lane == i, turned, block)
                blocks.append(block)
        return blocks

    def part_copy(number):
        return pltpu.make_async_remote_copy(
            src_ref=part_buf.at[number],
            dst_ref=sum_in.at[number],
            send_sem=psend_sem.at[number],
            recv_sem=precv_sem.at[number],
            device_id={"tm": 1 - core},
            device_id_type=MESH,
        )

    stage_tiles = half_tiles // STAGES
    stage_width = stage_tiles * 128

    def lanes_of(side, stage):
        start = (STAGES * side + stage) * stage_width
        return pl.ds(pl.multiple_of(start, stage_width), stage_width)

    def slot_of(source, side, stage):
        return out_ref.at[
            pl.ds(pl.multiple_of(source * COEFS, COEFS), COEFS), lanes_of(side, stage)
        ]

    def result_copy(number, source, stage):
        return pltpu.make_async_remote_copy(
            src_ref=res_buf.at[stage, number],
            dst_ref=slot_of(source, core, stage),
            send_sem=rsend_sem.at[stage, number],
            recv_sem=rrecv_sem.at[stage, source],
            device_id={"sta": number},
            device_id_type=MESH,
        )

    def forward_copy(source, side, stage):
        return pltpu.make_async_remote_copy(
            src_ref=slot_of(source, side, stage),
            dst_ref=slot_of(source, side, stage),
            send_sem=fsend_sem.at[stage, source],
            recv_sem=frecv_sem.at[stage, source],
            device_id={"tm": 1 - core},
            device_id_type=MESH,
        )

    def own_copy(stage):
        return pltpu.make_async_copy(
            res_buf.at[stage, me], slot_of(me, core, stage), own_sem.at[stage]
        )

    def stage_of(stage, carry):
        def theirs(number, carry):
            blocks = tile_of((1 - core) * half_tiles + number)
            for o in range(group_count):
                part_buf[number, o] = blocks[o].astype(BF16)
            part_copy(number).start()
            return carry

        lax.fori_loop(stage * stage_tiles, (stage + 1) * stage_tiles, theirs, 0)
        for n in range(stage_tiles):
            number = stage * stage_tiles + n
            blocks = tile_of(core * half_tiles + number)
            part_copy(number).wait_recv()
            for o in range(group_count):
                total = blocks[o] + sum_in[number, o].astype(F32)
                res_buf[stage, o, :, n * 128 : (n + 1) * 128] = total.astype(BF16)
        for step in range(group_count):
            there = (me + step + half) % group_count
            if step == half:
                own_copy(stage).start()
            else:
                result_copy(there, me, stage).start()
        return carry

    lax.fori_loop(0, STAGES, stage_of, 0)

    for stage in range(STAGES):
        own_copy(stage).wait()
        forward_copy(me, core, stage).start()
        for step in range(1, group_count):
            source = (me + step) % group_count
            result_copy(source, source, stage).wait_recv()
            forward_copy(source, core, stage).start()
    for stage in range(STAGES):
        for source in range(group_count):
            forward_copy(source, 1 - core, stage).wait_recv()
            forward_copy(source, core, stage).wait_send()
        for step in range(1, group_count):
            result_copy((me + step) % group_count, me, stage).wait_send()
    for step in range(1, group_count):
        bulk_copy((mine + step) % group_count, me).wait_send()
        index_copy(step).wait_send()
    for number in range(half_tiles):
        part_copy(number).wait_send()


def per_device(strain, masks, pair_local, pair_remote, owner):
    group_count = lax.axis_size("sta")
    time_count = lax.axis_size("tm")
    seg_count = strain.shape[0] // SEG_LEN
    channels = strain.shape[1]
    round_count, pair_count = pair_local.shape
    capacity = max(2, 2 * round_count * pair_count // group_count)
    slots = group_count * capacity
    bins = FREQS // group_count
    rows = seg_count * 2 * bins
    norm_scale = 1.0 / math.sqrt(seg_count * time_count * FREQS)
    left, right = inverse_factors(group_count, norm_scale)
    order = [slice_of(group, group_count) for group in range(group_count)]
    right = right.reshape(group_count, COEFS, LAGS)[np.array(order)].reshape(-1, LAGS)
    half_tiles = slots // 256
    pairs = round_count * pair_count
    lists = owner.reshape(1, pairs)
    for array in (pair_local, pair_remote, masks[None, :]):
        array = jnp.pad(array, ((0, 0), (0, pairs - array.shape[1])))
        lists = jnp.concatenate([lists, array])
    dma = pltpu.SemaphoreType.DMA
    vmem = pl.BlockSpec(memory_space=pltpu.VMEM)
    coefs = pl.pallas_call(
        functools.partial(main_kernel, group_count, capacity, seg_count, pair_local.shape),
        out_shape=jax.ShapeDtypeStruct((group_count * COEFS, slots), BF16),
        in_specs=[pl.BlockSpec(memory_space=pl.ANY)] * 2 + [vmem],
        out_specs=vmem,
        scratch_shapes=[
            pltpu.VMEM(((seg_count - 1) * SEG_LEN + SEG_PAD, channels), BF16),
            pltpu.VMEM((BLOCKS, 2 * BLOCK, SEG_PAD), BF16),
            pltpu.VMEM((2 * COEFS, 128), BF16),
            pltpu.SMEM((1, round_count * pair_count), jnp.int32),
            pltpu.VMEM((2 * COEFS * (128 // capacity), 2 * bins * (128 // capacity)), BF16),
            pltpu.VMEM((2, seg_count, 2 * BLOCK, channels), F32),
            pltpu.VMEM((seg_count, (BLOCKS + 2) * BLOCK, channels), BF16),
            pltpu.VMEM((seg_count, (BLOCKS + 2) * BLOCK, channels), BF16),
            pltpu.VMEM((channels, CHUNK), BF16),
            pltpu.VMEM((group_count, rows, channels), BF16),
            pltpu.VMEM((group_count, rows, channels), BF16),
            pltpu.VMEM((group_count, rows, slots), BF16),
            pltpu.VMEM((group_count, rows, slots), BF16),
            pltpu.VMEM((group_count, rows, slots), BF16),
            pltpu.VMEM((16, CHUNK // 2), BF16),
            pltpu.VMEM((2, group_count, 16, CHUNK // 2), BF16),
            pltpu.VMEM((half_tiles, group_count, COEFS, 128), BF16),
            pltpu.VMEM((half_tiles, group_count, COEFS, 128), BF16),
            pltpu.VMEM((STAGES, group_count, COEFS, half_tiles * 128 // STAGES), BF16),
            dma((2,)),
            dma((seg_count,)),
            dma((BLOCKS,)),
            dma((group_count,)),
            dma((group_count,)),
            dma((group_count,)),
            dma((group_count,)),
            dma((half_tiles,)),
            dma((half_tiles,)),
            dma((STAGES, group_count)),
            dma((STAGES, group_count)),
            dma((STAGES, group_count)),
            dma((STAGES, group_count)),
            dma((STAGES,)),
        ],
        compiler_params=pltpu.CompilerParams(
            collective_id=0, has_side_effects=True, vmem_limit_bytes=48 * 1024 * 1024
        ),
    )(strain, jnp.asarray(tables(left)), lists)
    width = LAGS // time_count
    mine = lax.dynamic_slice_in_dim(
        jnp.asarray(right), lax.axis_index("tm") * width, width, axis=1
    )
    return jnp.einsum("cs,cl->sl", coefs, mine, preferred_element_type=F32)


def solution(mesh):
    placed = (P("tm", "sta"), P(), P(None, "sta"), P(None, "sta"), P("sta", None))
    return jax.shard_map(
        per_device, mesh=mesh, in_specs=placed, out_specs=P("sta", "tm"), check_vma=False
    )
```

```python
import functools
import math

import jax
import jax.numpy as jnp
import ml_dtypes
import numpy as np
from jax import lax
from jax.experimental import pallas as pl
from jax.experimental.pallas import tpu as pltpu
from jax.sharding import PartitionSpec as P

SEG_LEN = 6000
SEG_PAD = 6144
FREQS = 512
WIN = 32
LAGS = 512
EPSILON = 1e-06
BLOCK = 64
BLOCKS = FREQS // BLOCK
CHUNK = 256
COEFS = 16
STAGES = 2
LEFT_ROW = SEG_PAD // 128
F32 = jnp.float32
BF16 = jnp.bfloat16
MESH = pl.DeviceIdType.MESH


def angles_of(product):
    return np.mod(product, SEG_LEN).astype(np.float32) * np.float32(2.0 * math.pi / SEG_LEN)


def forward_blocks():
    angles = angles_of(np.arange(1, FREQS + 1)[:, None] * np.arange(SEG_LEN)[None, :])
    table = np.zeros((BLOCKS, 2, BLOCK, SEG_PAD), np.float32)
    table[:, 0, :, :SEG_LEN] = np.cos(angles).reshape(BLOCKS, BLOCK, SEG_LEN)
    table[:, 1, :, :SEG_LEN] = -np.sin(angles).reshape(BLOCKS, BLOCK, SEG_LEN)
    return table.reshape(BLOCKS, 2 * BLOCK, SEG_PAD).astype(ml_dtypes.bfloat16)


def inverse_factors(slices, scale):
    angles = angles_of(np.arange(1, FREQS + 1)[:, None] * (np.arange(LAGS) - LAGS // 2)[None, :])
    angles = angles.astype(np.float64)
    bins = FREQS // slices
    left, right = [], []
    for number in range(slices):
        part = angles[number * bins : (number + 1) * bins]
        u, s, vt = np.linalg.svd(np.concatenate([np.cos(part), -np.sin(part)]), full_matrices=False)
        left.append(u[:, :COEFS].T)
        right.append(s[:COEFS, None] * vt[:COEFS] * scale)
    left = np.stack(left).astype(np.float32)
    high = left.astype(ml_dtypes.bfloat16)
    low = (left - high.astype(np.float32)).astype(ml_dtypes.bfloat16)
    return np.concatenate([high, low], axis=1), np.concatenate(right).astype(ml_dtypes.bfloat16)


def tables(left):
    last = np.zeros((2 * BLOCK, SEG_PAD), ml_dtypes.bfloat16)
    for number, block in enumerate(left):
        row, col = number // LEFT_ROW * 2 * COEFS, number % LEFT_ROW * 128
        last[row : row + 2 * COEFS, col : col + block.shape[1]] = block
    return np.concatenate([forward_blocks(), last[None]])


def home_of(number, group_count):
    half, quarter = group_count // 2, group_count // 4
    odd = number % 2
    return number // half * half + odd * quarter + ((number % half // 2) ^ (odd * (quarter - 1)))


def slice_of(group, group_count):
    half, quarter = group_count // 2, group_count // 4
    odd = group // quarter % 2
    return group // half * half + 2 * ((group % quarter) ^ (odd * (quarter - 1))) + odd


def dot(left, right):
    return jnp.dot(left, right, preferred_element_type=F32)


def main_kernel(
    group_count, capacity, seg_count, pair_shape,
    strain_hbm, table_hbm, lists_ref,
    out_ref,
    strain_buf, table_buf, left_ref, masks_ref, wide_ref,
    spec_buf, high_buf, low_buf, iota_buf, sent_buf, got_buf,
    near_buf, full_buf, other_buf,
    index_out, index_buf, part_buf, sum_in, res_buf,
    small_sem, strain_sem, table_sem, send_sem, recv_sem, isend_sem, irecv_sem,
    psend_sem, precv_sem, rsend_sem, rrecv_sem, fsend_sem, frecv_sem, own_sem,
):
    round_count, pair_count = pair_shape
    pairs = round_count * pair_count
    bins = FREQS // group_count
    per_block = BLOCK // bins
    rows = 2 * bins
    slots = group_count * capacity
    chunks = slots // CHUNK
    channels = strain_hbm.shape[1]
    half, quarter = group_count // 2, group_count // 4
    full_mask = group_count - 1
    me, core = lax.axis_index("sta"), lax.axis_index("tm")
    upper = me >= half
    mine = slice_of(me, group_count)
    near_base = jnp.where(upper, half, 0)
    far_base = half - near_base

    mask_row = 1 + 2 * round_count
    masks_copy = pltpu.make_async_copy(lists_ref.at[pl.ds(mask_row, 1)], masks_ref, small_sem.at[0])
    masks_copy.start()
    left_copy = pltpu.make_async_copy(
        table_hbm.at[
            BLOCKS,
            pl.ds(pl.multiple_of(mine // LEFT_ROW * 2 * COEFS, 2 * COEFS), 2 * COEFS),
            pl.ds(pl.multiple_of(mine % LEFT_ROW * 128, 128), 128),
        ],
        left_ref,
        small_sem.at[1],
    )
    left_copy.start()
    ends = [min(seg * SEG_LEN + SEG_PAD, seg_count * SEG_LEN) for seg in range(seg_count)]
    strain_copies = []
    for seg, (low, high) in enumerate(zip([0] + ends[:-1], ends)):
        place = pl.ds(low, high - low)
        strain_copies.append(
            pltpu.make_async_copy(strain_hbm.at[place], strain_buf.at[place], strain_sem.at[seg])
        )

    def block_of(step):
        return jnp.where(upper, step, BLOCKS - 1 - step)

    def table_copy(step):
        return pltpu.make_async_copy(
            table_hbm.at[block_of(step)], table_buf.at[step], table_sem.at[step]
        )

    strain_copies[0].start()
    table_copy(0).start()
    table_copy(1).start()
    for copy in strain_copies[1:]:
        copy.start()

    barrier = pltpu.get_barrier_semaphore()
    for step in range(1, group_count):
        pl.semaphore_signal(
            barrier, inc=1, device_id={"sta": (me + step) % group_count}, device_id_type=MESH
        )
    pl.semaphore_signal(barrier, inc=1, device_id={"tm": 1 - core}, device_id_type=MESH)

    tail = strain_buf.shape[0] - seg_count * SEG_LEN
    strain_buf[pl.ds(seg_count * SEG_LEN, tail), :] = jnp.zeros((tail, channels), BF16)
    edge = jnp.zeros((BLOCK, channels), BF16)
    for seg in range(seg_count):
        for buf in (high_buf, low_buf):
            buf[seg, pl.ds(0, BLOCK), :] = edge
            buf[seg, pl.ds((BLOCKS + 1) * BLOCK, BLOCK), :] = edge
    numbers = lax.broadcasted_iota(jnp.int32, (channels, CHUNK), 0) + 1
    iota_buf[...] = numbers.astype(F32).astype(BF16)


    def index_copy(step):
        there = (me + step) % group_count
        return pltpu.make_async_remote_copy(
            src_ref=index_out,
            dst_ref=index_buf.at[core, me],
            send_sem=isend_sem.at[step - 1],
            recv_sem=irecv_sem.at[step - 1],
            device_id={"sta": there},
            device_id_type=MESH,
        )

    masks_copy.wait()
    left_copy.wait()

    def one_row(first):
        return jnp.concatenate(
            [lists_ref[first + r : first + r + 1, :pair_count] for r in range(round_count)], axis=1
        )

    owners = lists_ref[0:1, :]
    hot = (owners == lax.broadcasted_iota(jnp.int32, (group_count, pairs), 0)).astype(F32)
    before = lax.broadcasted_iota(jnp.int32, (pairs, pairs), 0) < lax.broadcasted_iota(
        jnp.int32, (pairs, pairs), 1
    )
    earlier = dot(hot.astype(BF16), before.astype(F32).astype(BF16))
    slot = jnp.sum(earlier * hot, axis=0, keepdims=True).astype(jnp.int32)
    target = owners * capacity + slot
    placed = (target == lax.broadcasted_iota(jnp.int32, (slots, pairs), 0)).astype(F32).astype(BF16)
    kind = lax.broadcasted_iota(jnp.int32, (8, pairs), 0) % 4
    turn = lax.broadcasted_iota(jnp.int32, (8, pairs), 1) // pair_count
    first_kind = jnp.where(masks_ref[0, 0] == full_mask, 1, 2)
    far_kind = jnp.where(turn == 0, first_kind, 3 - first_kind)
    near, far = one_row(1) + 1, one_row(1 + round_count) + 1
    listed = jnp.where(kind == 0, near, jnp.where(kind == far_kind, far, 0))
    ordered = lax.dot_general(
        listed.astype(F32).astype(BF16),
        placed,
        (((1,), (1,)), ((), ())),
        preferred_element_type=F32,
    )
    first = lax.broadcasted_iota(jnp.int32, (8, CHUNK), 0) < 4
    tiles = []
    for chunk in range(0, chunks, 2):
        even = ordered[:, chunk * CHUNK : (chunk + 1) * CHUNK]
        odd = ordered[:, (chunk + 1) * CHUNK : (chunk + 2) * CHUNK]
        tiles.append(jnp.where(first, even, odd))
    own_index = jnp.concatenate(tiles, axis=0).astype(BF16)
    own_index = jnp.where(core == 0, own_index[:, :128], own_index[:, 128:])
    index_out[...] = own_index
    index_buf[core, me] = own_index
    def index_share():
        place = index_buf.at[core]
        return pltpu.make_async_remote_copy(
            src_ref=place,
            dst_ref=place,
            send_sem=isend_sem.at[group_count - 1],
            recv_sem=irecv_sem.at[group_count - 1],
            device_id={"tm": 1 - core},
            device_id_type=MESH,
        )

    pl.semaphore_wait(barrier, group_count)
    for step in range(1, group_count):
        index_copy(step).start()

    band_row = lax.broadcasted_iota(jnp.int32, (BLOCK, 3 * BLOCK), 0) + BLOCK
    band_col = lax.broadcasted_iota(jnp.int32, (BLOCK, 3 * BLOCK), 1)
    band = (jnp.abs(band_row - band_col) <= WIN).astype(F32).astype(BF16)

    def transform_segment(step, seg):
        spectra = dot(table_buf[step], strain_buf[pl.ds(seg * SEG_LEN, SEG_PAD), :])
        spec_buf[step % 2, seg] = spectra
        real, imag = spectra[:BLOCK], spectra[BLOCK:]
        amplitude = jnp.sqrt(real * real + imag * imag)
        high = amplitude.astype(BF16)
        place = pl.ds(pl.multiple_of((block_of(step) + 1) * BLOCK, BLOCK), BLOCK)
        high_buf[seg, place, :] = high
        low_buf[seg, place, :] = (amplitude - high.astype(F32)).astype(BF16)

    def transform(step):
        table_copy(step).wait()

        @pl.when(step + 2 < BLOCKS)
        def _():
            table_copy(step + 2).start()

        for seg in range(seg_count):
            transform_segment(step, seg)

    def bulk_copy(number, source):
        return pltpu.make_async_remote_copy(
            src_ref=sent_buf.at[number],
            dst_ref=got_buf.at[source],
            send_sem=send_sem.at[number],
            recv_sem=recv_sem.at[source],
            device_id={"sta": home_of(number, group_count)},
            device_id_type=MESH,
        )

    def whiten_segment(step, seg):
        block = block_of(step)
        around = pl.ds(pl.multiple_of(block * BLOCK, BLOCK), 3 * BLOCK)
        total = dot(band, high_buf[seg, around, :]) + dot(band, low_buf[seg, around, :])
        inverse = 1.0 / (total * (1.0 / (2 * WIN + 1)) + EPSILON)
        for part in range(per_block):
            inside = inverse[part * bins : (part + 1) * bins]
            real = spec_buf[step % 2, seg, part * bins : (part + 1) * bins, :] * inside
            imag = spec_buf[step % 2, seg, BLOCK + part * bins : BLOCK + (part + 1) * bins, :]
            both = jnp.concatenate([real, imag * inside], axis=0).astype(BF16)
            sent_buf[block * per_block + part, seg * rows : (seg + 1) * rows, :] = both

    def piece_copy(number, seg):
        place = pl.ds(seg * rows, rows)
        return pltpu.make_async_remote_copy(
            src_ref=sent_buf.at[number, place],
            dst_ref=got_buf.at[me, place],
            send_sem=send_sem.at[number],
            recv_sem=recv_sem.at[me],
            device_id={"sta": home_of(number, group_count)},
            device_id_type=MESH,
        )

    def whiten(step):
        block = block_of(step)
        for seg in range(seg_count):
            whiten_segment(step, seg)

        @pl.when(step == 1)
        def _():
            for part in range(per_block):
                bulk_copy(block * per_block + part, me).start()

        @pl.when(step == 3)
        def _():
            base = jnp.where(upper, quarter, half)
            for part in range(quarter):
                bulk_copy(base + (me + part) % quarter, me).start()

        @pl.when(step >= 4)
        def _():
            for part in range(per_block):
                number = block * per_block + part

                @pl.when(number != mine)
                def _():
                    bulk_copy(number, me).start()

                @pl.when(number == mine)
                def _():
                    got_buf[me] = sent_buf[mine]

    for step in range(2):
        table_copy(step).wait()
    for seg in range(seg_count):
        strain_copies[seg].wait()
        if seg == 1:
            for step in range(2, 4):
                table_copy(step).start()
        transform_segment(0, seg)
        transform_segment(1, seg)
        whiten_segment(0, seg)
        for part in range(per_block):
            piece_copy(block_of(0) * per_block + part, seg).start()


    def body(step, carry):
        transform(step)
        whiten(step - 1)
        return carry

    lax.fori_loop(2, BLOCKS, body, 0)
    for step in range(1, group_count):
        index_copy(step).wait_recv()
    index_share().start()
    whiten(BLOCKS - 1)
    index_share().wait()

    one, zero = jnp.ones((channels, CHUNK), BF16), jnp.zeros((channels, CHUNK), BF16)
    other_mask = masks_ref[0, 0] ^ masks_ref[0, 1] ^ full_mask
    other_mask = jnp.bitwise_and(other_mask, full_mask)

    def index_of(group):
        return jnp.concatenate([index_buf[0, group], index_buf[1, group]], axis=1)

    def pick(source):
        block = got_buf[source]
        partner = full_mask - source
        listed = [
            index_of(source),
            index_of(partner),
            index_of(jnp.bitwise_xor(source, other_mask)),
        ]
        places = [near_buf.at[source], full_buf.at[partner], other_buf.at[source]]
        for chunk in range(chunks):
            for n in range(3):
                row = listed[n][4 * chunk + n : 4 * chunk + n + 1]
                chosen = dot(block, jnp.where(iota_buf[...] == row, one, zero))
                places[n][:, chunk * CHUNK : (chunk + 1) * CHUNK] = chosen.astype(BF16)

    def near_group(number, carry):
        source = near_base + (me + number) % half

        @pl.when(source != me)
        def _():
            bulk_copy(source, source).wait_recv()

        pick(source)
        return carry

    def far_group(number, carry):
        source = far_base + (mine - number // 2 + group_count) % quarter + quarter * (number % 2)
        bulk_copy(source, source).wait_recv()
        pick(source)
        return carry

    lax.fori_loop(0, half, near_group, 0)
    lax.fori_loop(0, half, far_group, 0)

    def part_of(shape, axis, size, number):
        return (lax.broadcasted_iota(jnp.int32, shape, axis) // size == number).astype(F32)

    per_tile = 128 // capacity
    group_tiles = group_count // per_tile
    half_tiles = group_tiles // 2
    lane = lax.broadcasted_iota(jnp.int32, (COEFS, 128), 1) // capacity
    tall = jnp.concatenate([left_ref[...].astype(F32)] * per_tile, axis=0)
    widest = sum(
        pltpu.roll(tall, rows * i, 1) * (part_of(tall.shape, 0, 2 * COEFS, i)) for i in range(per_tile)
    )
    wide_ref[...] = widest[:, : rows * per_tile].astype(BF16)

    def cross_of(group, lanes):
        peer = jnp.bitwise_xor(group, other_mask)
        real, imag = 0.0, 0.0
        for seg in range(seg_count):
            low = seg * rows
            a = near_buf[group, low : low + rows, lanes].astype(F32)
            b = full_buf[group, low : low + rows, lanes]
            b = (b + other_buf[peer, low : low + rows, lanes]).astype(F32)
            ar, ai, br, bi = a[:bins], a[bins:], b[:bins], b[bins:]
            real = real + (ar * br + ai * bi)
            imag = imag + (ai * br - ar * bi)
        return jnp.concatenate([real, imag], axis=0).astype(BF16)

    def tile_of(tile):
        found = [[] for _ in range(per_tile)]
        for chunk in range(chunks):
            lanes = slice(chunk * CHUNK, (chunk + 1) * CHUNK)
            cross = [cross_of(tile * per_tile + i, lanes) for i in range(per_tile)]
            both = dot(wide_ref[...], jnp.concatenate(cross, axis=0))
            for i in range(per_tile):
                part = both[2 * COEFS * i : 2 * COEFS * (i + 1)]
                found[i].append(part[:COEFS] + part[COEFS:])
        parts = [jnp.concatenate(f, axis=1) for f in found]
        blocks = []
        for owner_tile in range(slots // 128):
            cut = [p[:, owner_tile * 128 : (owner_tile + 1) * 128] for p in parts]
            for o in range(per_tile):
                block = cut[0] if o == 0 else pltpu.roll(cut[0], (128 - o * capacity) % 128, 1)
                for i in range(1, per_tile):
                    turned = cut[i]
                    if i != o:
                        turned = pltpu.roll(turned, ((i - o) * capacity) % 128, 1)
                    block = jnp.where(lane == i, turned, block)
                blocks.append(block)
        return blocks

    def part_copy(number):
        return pltpu.make_async_remote_copy(
            src_ref=part_buf.at[number],
            dst_ref=sum_in.at[number],
            send_sem=psend_sem.at[number],
            recv_sem=precv_sem.at[number],
            device_id={"tm": 1 - core},
            device_id_type=MESH,
        )

    stage_tiles = half_tiles // STAGES
    stage_width = stage_tiles * 128

    def lanes_of(side, stage):
        start = (STAGES * side + stage) * stage_width
        return pl.ds(pl.multiple_of(start, stage_width), stage_width)

    def slot_of(source, side, stage):
        return out_ref.at[
            pl.ds(pl.multiple_of(source * COEFS, COEFS), COEFS), lanes_of(side, stage)
        ]

    def result_copy(number, stage, side):
        return pltpu.make_async_remote_copy(
            src_ref=res_buf.at[stage, number],
            dst_ref=slot_of(me, core, stage),
            send_sem=rsend_sem.at[stage],
            recv_sem=rrecv_sem.at[stage, side],
            device_id={"sta": number},
            device_id_type=MESH,
        )

    def arrived(stage, side, count):
        place = out_ref.at[pl.ds(0, count * COEFS), lanes_of(core, stage)]
        return pltpu.make_async_remote_copy(
            src_ref=place,
            dst_ref=place,
            send_sem=rsend_sem.at[stage],
            recv_sem=rrecv_sem.at[stage, side],
            device_id={"sta": far_base},
            device_id_type=MESH,
        )

    def forward_copy(base, count, side, stage):
        rows = pl.ds(pl.multiple_of(base * COEFS, COEFS), count * COEFS)
        place = out_ref.at[rows, lanes_of(side, stage)]
        return pltpu.make_async_remote_copy(
            src_ref=place,
            dst_ref=place,
            send_sem=fsend_sem.at[stage],
            recv_sem=frecv_sem.at[stage],
            device_id={"tm": 1 - core},
            device_id_type=MESH,
        )

    def own_copy(stage):
        return pltpu.make_async_copy(
            res_buf.at[stage, me], slot_of(me, core, stage), own_sem.at[stage]
        )

    def stage_of(stage, carry):
        def theirs(number, carry):
            blocks = tile_of((1 - core) * half_tiles + number)
            for o in range(group_count):
                part_buf[number, o] = blocks[o].astype(BF16)
            part_copy(number).start()
            return carry

        lax.fori_loop(stage * stage_tiles, (stage + 1) * stage_tiles, theirs, 0)
        for n in range(stage_tiles):
            number = stage * stage_tiles + n
            blocks = tile_of(core * half_tiles + number)
            part_copy(number).wait_recv()
            for o in range(group_count):
                total = blocks[o] + sum_in[number, o].astype(F32)
                res_buf[stage, o, :, n * 128 : (n + 1) * 128] = total.astype(BF16)
        for step in range(half):
            result_copy(far_base + (me + step) % half, stage, 1).start()
        own_copy(stage).start()
        for step in range(1, half):
            result_copy(near_base + (me + step) % half, stage, 0).start()
        return carry

    lax.fori_loop(0, STAGES, stage_of, 0)

    for step in range(1, group_count):
        bulk_copy((mine + step) % group_count, me).wait_send()
        index_copy(step).wait_send()
    for number in range(half_tiles):
        part_copy(number).wait_send()
    for stage in range(STAGES):
        own_copy(stage).wait()
        arrived(stage, 0, half - 1).wait_recv()
        forward_copy(near_base, half, core, stage).start()
        arrived(stage, 1, half).wait_recv()
        forward_copy(far_base, half, core, stage).start()
    for stage in range(STAGES):
        arrived(stage, 1, group_count - 1).wait_send()
    for stage in range(STAGES):
        forward_copy(0, group_count, core, stage).wait_send()
        forward_copy(0, group_count, 1 - core, stage).wait_recv()


def per_device(strain, masks, pair_local, pair_remote, owner):
    group_count = lax.axis_size("sta")
    time_count = lax.axis_size("tm")
    seg_count = strain.shape[0] // SEG_LEN
    channels = strain.shape[1]
    round_count, pair_count = pair_local.shape
    capacity = max(2, 2 * round_count * pair_count // group_count)
    slots = group_count * capacity
    bins = FREQS // group_count
    rows = seg_count * 2 * bins
    norm_scale = 1.0 / math.sqrt(seg_count * time_count * FREQS)
    left, right = inverse_factors(group_count, norm_scale)
    order = [slice_of(group, group_count) for group in range(group_count)]
    right = right.reshape(group_count, COEFS, LAGS)[np.array(order)].reshape(-1, LAGS)
    half_tiles = slots // 256
    pairs = round_count * pair_count
    lists = owner.reshape(1, pairs)
    for array in (pair_local, pair_remote, masks[None, :]):
        array = jnp.pad(array, ((0, 0), (0, pairs - array.shape[1])))
        lists = jnp.concatenate([lists, array])
    dma = pltpu.SemaphoreType.DMA
    vmem = pl.BlockSpec(memory_space=pltpu.VMEM)
    coefs = pl.pallas_call(
        functools.partial(main_kernel, group_count, capacity, seg_count, pair_local.shape),
        out_shape=jax.ShapeDtypeStruct((group_count * COEFS, slots), BF16),
        in_specs=[pl.BlockSpec(memory_space=pl.ANY)] * 2 + [vmem],
        out_specs=vmem,
        scratch_shapes=[
            pltpu.VMEM(((seg_count - 1) * SEG_LEN + SEG_PAD, channels), BF16),
            pltpu.VMEM((BLOCKS, 2 * BLOCK, SEG_PAD), BF16),
            pltpu.VMEM((2 * COEFS, 128), BF16),
            pltpu.SMEM((1, round_count * pair_count), jnp.int32),
            pltpu.VMEM((2 * COEFS * (128 // capacity), 2 * bins * (128 // capacity)), BF16),
            pltpu.VMEM((2, seg_count, 2 * BLOCK, channels), F32),
            pltpu.VMEM((seg_count, (BLOCKS + 2) * BLOCK, channels), BF16),
            pltpu.VMEM((seg_count, (BLOCKS + 2) * BLOCK, channels), BF16),
            pltpu.VMEM((channels, CHUNK), BF16),
            pltpu.VMEM((group_count, rows, channels), BF16),
            pltpu.VMEM((group_count, rows, channels), BF16),
            pltpu.VMEM((group_count, rows, slots), BF16),
            pltpu.VMEM((group_count, rows, slots), BF16),
            pltpu.VMEM((group_count, rows, slots), BF16),
            pltpu.VMEM((16, CHUNK // 2), BF16),
            pltpu.VMEM((2, group_count, 16, CHUNK // 2), BF16),
            pltpu.VMEM((half_tiles, group_count, COEFS, 128), BF16),
            pltpu.VMEM((half_tiles, group_count, COEFS, 128), BF16),
            pltpu.VMEM((STAGES, group_count, COEFS, half_tiles * 128 // STAGES), BF16),
            dma((2,)),
            dma((seg_count,)),
            dma((BLOCKS,)),
            dma((group_count,)),
            dma((group_count,)),
            dma((group_count,)),
            dma((group_count,)),
            dma((half_tiles,)),
            dma((half_tiles,)),
            dma((STAGES,)),
            dma((STAGES, 2)),
            dma((STAGES,)),
            dma((STAGES,)),
            dma((STAGES,)),
        ],
        compiler_params=pltpu.CompilerParams(
            collective_id=0, has_side_effects=True, vmem_limit_bytes=48 * 1024 * 1024
        ),
    )(strain, jnp.asarray(tables(left)), lists)
    width = LAGS // time_count
    mine = lax.dynamic_slice_in_dim(
        jnp.asarray(right), lax.axis_index("tm") * width, width, axis=1
    )
    return jnp.einsum("cs,cl->sl", coefs, mine, preferred_element_type=F32)


def solution(mesh):
    placed = (P("tm", "sta"), P(), P(None, "sta"), P(None, "sta"), P("sta", None))
    return jax.shard_map(
        per_device, mesh=mesh, in_specs=placed, out_specs=P("sta", "tm"), check_vma=False
    )
```

```python
import functools
import math

import jax
import jax.numpy as jnp
import ml_dtypes
import numpy as np
from jax import lax
from jax.experimental import pallas as pl
from jax.experimental.pallas import tpu as pltpu
from jax.sharding import PartitionSpec as P

SEG_LEN = 6000
SEG_PAD = 6144
FREQS = 512
WIN = 32
LAGS = 512
EPSILON = 1e-06
BLOCK = 64
BLOCKS = FREQS // BLOCK
CHUNK = 256
COEFS = 24
STAGES = 2
LEFT_ROW = SEG_PAD // 128
F32 = jnp.float32
BF16 = jnp.bfloat16
MESH = pl.DeviceIdType.MESH


def angles_of(product):
    return np.mod(product, SEG_LEN).astype(np.float32) * np.float32(2.0 * math.pi / SEG_LEN)


def forward_blocks():
    angles = angles_of(np.arange(1, FREQS + 1)[:, None] * np.arange(SEG_LEN)[None, :])
    table = np.zeros((BLOCKS, 2, BLOCK, SEG_PAD), np.float32)
    table[:, 0, :, :SEG_LEN] = np.cos(angles).reshape(BLOCKS, BLOCK, SEG_LEN)
    table[:, 1, :, :SEG_LEN] = -np.sin(angles).reshape(BLOCKS, BLOCK, SEG_LEN)
    return table.reshape(BLOCKS, 2 * BLOCK, SEG_PAD).astype(ml_dtypes.bfloat16)


def inverse_factors(slices, scale):
    angles = angles_of(np.arange(1, FREQS + 1)[:, None] * (np.arange(LAGS) - LAGS // 2)[None, :])
    angles = angles.astype(np.float64)
    bins = FREQS // slices
    coefs = min(COEFS, 2 * bins)
    left, right = [], []
    for number in range(slices):
        part = angles[number * bins : (number + 1) * bins]
        u, s, vt = np.linalg.svd(np.concatenate([np.cos(part), -np.sin(part)]), full_matrices=False)
        left.append(u[:, :coefs].T)
        right.append(s[:coefs, None] * vt[:coefs] * scale)
    left = np.stack(left).astype(np.float32)
    high = left.astype(ml_dtypes.bfloat16)
    low = (left - high.astype(np.float32)).astype(ml_dtypes.bfloat16)
    return np.concatenate([high, low], axis=1), np.concatenate(right).astype(ml_dtypes.bfloat16)


def tables(left):
    last = np.zeros((2 * BLOCK, SEG_PAD), ml_dtypes.bfloat16)
    for number, block in enumerate(left):
        row, col = number // LEFT_ROW * len(block), number % LEFT_ROW * 128
        last[row : row + len(block), col : col + block.shape[1]] = block
    return np.concatenate([forward_blocks(), last[None]])


def home_of(number, group_count):
    half, quarter = group_count // 2, group_count // 4
    odd = number % 2
    return number // half * half + odd * quarter + ((number % half // 2) ^ (odd * (quarter - 1)))


def slice_of(group, group_count):
    half, quarter = group_count // 2, group_count // 4
    odd = group // quarter % 2
    return group // half * half + 2 * ((group % quarter) ^ (odd * (quarter - 1))) + odd


def dot(left, right):
    return jnp.dot(left, right, preferred_element_type=F32)


def main_kernel(
    group_count, capacity, seg_count, pair_shape,
    strain_hbm, table_hbm, lists_ref,
    out_ref,
    strain_buf, table_buf, left_ref, masks_ref, wide_ref,
    spec_buf, high_buf, low_buf, iota_buf, sent_buf, got_buf,
    near_buf, full_buf, other_buf,
    index_out, index_buf, part_buf, sum_in, res_buf,
    small_sem, strain_sem, table_sem, send_sem, recv_sem, isend_sem, irecv_sem,
    psend_sem, precv_sem, rsend_sem, rrecv_sem, fsend_sem, frecv_sem, own_sem,
):
    round_count, pair_count = pair_shape
    pairs = round_count * pair_count
    bins = FREQS // group_count
    per_block = BLOCK // bins
    rows = 2 * bins
    coefs = min(COEFS, rows)
    slots = group_count * capacity
    chunks = slots // CHUNK
    channels = strain_hbm.shape[1]
    half, quarter = group_count // 2, group_count // 4
    full_mask = group_count - 1
    me, core = lax.axis_index("sta"), lax.axis_index("tm")
    upper = me >= half
    mine = slice_of(me, group_count)
    near_base = jnp.where(upper, half, 0)
    far_base = half - near_base

    mask_row = 1 + 2 * round_count
    masks_copy = pltpu.make_async_copy(lists_ref.at[pl.ds(mask_row, 1)], masks_ref, small_sem.at[0])
    masks_copy.start()
    left_copy = pltpu.make_async_copy(
        table_hbm.at[
            BLOCKS,
            pl.ds(pl.multiple_of(mine // LEFT_ROW * 2 * coefs, 2 * coefs), 2 * coefs),
            pl.ds(pl.multiple_of(mine % LEFT_ROW * 128, 128), 128),
        ],
        left_ref,
        small_sem.at[1],
    )
    left_copy.start()
    ends = [min(seg * SEG_LEN + SEG_PAD, seg_count * SEG_LEN) for seg in range(seg_count)]
    strain_copies = []
    for seg, (low, high) in enumerate(zip([0] + ends[:-1], ends)):
        place = pl.ds(low, high - low)
        strain_copies.append(
            pltpu.make_async_copy(strain_hbm.at[place], strain_buf.at[place], strain_sem.at[seg])
        )

    def block_of(step):
        return jnp.where(upper, step, BLOCKS - 1 - step)

    def table_copy(step):
        return pltpu.make_async_copy(
            table_hbm.at[block_of(step)], table_buf.at[step], table_sem.at[step]
        )

    strain_copies[0].start()
    table_copy(0).start()
    table_copy(1).start()
    for copy in strain_copies[1:]:
        copy.start()

    barrier = pltpu.get_barrier_semaphore()
    for step in range(1, group_count):
        pl.semaphore_signal(
            barrier, inc=1, device_id={"sta": (me + step) % group_count}, device_id_type=MESH
        )
    pl.semaphore_signal(barrier, inc=1, device_id={"tm": 1 - core}, device_id_type=MESH)

    tail = strain_buf.shape[0] - seg_count * SEG_LEN
    strain_buf[pl.ds(seg_count * SEG_LEN, tail), :] = jnp.zeros((tail, channels), BF16)
    edge = jnp.zeros((BLOCK, channels), BF16)
    for seg in range(seg_count):
        for buf in (high_buf, low_buf):
            buf[seg, pl.ds(0, BLOCK), :] = edge
            buf[seg, pl.ds((BLOCKS + 1) * BLOCK, BLOCK), :] = edge
    numbers = lax.broadcasted_iota(jnp.int32, (channels, CHUNK), 0) + 1
    iota_buf[...] = numbers.astype(F32).astype(BF16)


    def index_copy(step):
        there = (me + step) % group_count
        return pltpu.make_async_remote_copy(
            src_ref=index_out,
            dst_ref=index_buf.at[core, me],
            send_sem=isend_sem.at[step - 1],
            recv_sem=irecv_sem.at[step - 1],
            device_id={"sta": there},
            device_id_type=MESH,
        )

    masks_copy.wait()
    left_copy.wait()

    def one_row(first):
        return jnp.concatenate(
            [lists_ref[first + r : first + r + 1, :pair_count] for r in range(round_count)], axis=1
        )

    owners = lists_ref[0:1, :]
    hot = (owners == lax.broadcasted_iota(jnp.int32, (group_count, pairs), 0)).astype(F32)
    before = lax.broadcasted_iota(jnp.int32, (pairs, pairs), 0) < lax.broadcasted_iota(
        jnp.int32, (pairs, pairs), 1
    )
    earlier = dot(hot.astype(BF16), before.astype(F32).astype(BF16))
    slot = jnp.sum(earlier * hot, axis=0, keepdims=True).astype(jnp.int32)
    target = owners * capacity + slot
    placed = (target == lax.broadcasted_iota(jnp.int32, (slots, pairs), 0)).astype(F32).astype(BF16)
    kind = lax.broadcasted_iota(jnp.int32, (8, pairs), 0) % 4
    turn = lax.broadcasted_iota(jnp.int32, (8, pairs), 1) // pair_count
    first_kind = jnp.where(masks_ref[0, 0] == full_mask, 1, 2)
    far_kind = jnp.where(turn == 0, first_kind, 3 - first_kind)
    near, far = one_row(1) + 1, one_row(1 + round_count) + 1
    listed = jnp.where(kind == 0, near, jnp.where(kind == far_kind, far, 0))
    ordered = lax.dot_general(
        listed.astype(F32).astype(BF16),
        placed,
        (((1,), (1,)), ((), ())),
        preferred_element_type=F32,
    )
    first = lax.broadcasted_iota(jnp.int32, (8, CHUNK), 0) < 4
    tiles = []
    for chunk in range(0, chunks, 2):
        even = ordered[:, chunk * CHUNK : (chunk + 1) * CHUNK]
        odd = ordered[:, (chunk + 1) * CHUNK : (chunk + 2) * CHUNK]
        tiles.append(jnp.where(first, even, odd))
    own_index = jnp.concatenate(tiles, axis=0).astype(BF16)
    own_index = jnp.where(core == 0, own_index[:, :128], own_index[:, 128:])
    index_out[...] = own_index
    index_buf[core, me] = own_index
    def index_share():
        place = index_buf.at[core]
        return pltpu.make_async_remote_copy(
            src_ref=place,
            dst_ref=place,
            send_sem=isend_sem.at[group_count - 1],
            recv_sem=irecv_sem.at[group_count - 1],
            device_id={"tm": 1 - core},
            device_id_type=MESH,
        )

    pl.semaphore_wait(barrier, group_count)
    for step in range(1, group_count):
        index_copy(step).start()

    band_row = lax.broadcasted_iota(jnp.int32, (BLOCK, 3 * BLOCK), 0) + BLOCK
    band_col = lax.broadcasted_iota(jnp.int32, (BLOCK, 3 * BLOCK), 1)
    band = (jnp.abs(band_row - band_col) <= WIN).astype(F32).astype(BF16)

    def transform_segment(step, seg):
        spectra = dot(table_buf[step], strain_buf[pl.ds(seg * SEG_LEN, SEG_PAD), :])
        spec_buf[step % 2, seg] = spectra
        real, imag = spectra[:BLOCK], spectra[BLOCK:]
        amplitude = jnp.sqrt(real * real + imag * imag)
        high = amplitude.astype(BF16)
        place = pl.ds(pl.multiple_of((block_of(step) + 1) * BLOCK, BLOCK), BLOCK)
        high_buf[seg, place, :] = high
        low_buf[seg, place, :] = (amplitude - high.astype(F32)).astype(BF16)

    def transform(step):
        table_copy(step).wait()

        @pl.when(step + 2 < BLOCKS)
        def _():
            table_copy(step + 2).start()

        for seg in range(seg_count):
            transform_segment(step, seg)

    def bulk_copy(number, source):
        return pltpu.make_async_remote_copy(
            src_ref=sent_buf.at[number],
            dst_ref=got_buf.at[source],
            send_sem=send_sem.at[number],
            recv_sem=recv_sem.at[source],
            device_id={"sta": home_of(number, group_count)},
            device_id_type=MESH,
        )

    def whiten_segment(step, seg):
        block = block_of(step)
        around = pl.ds(pl.multiple_of(block * BLOCK, BLOCK), 3 * BLOCK)
        total = dot(band, high_buf[seg, around, :]) + dot(band, low_buf[seg, around, :])
        inverse = 1.0 / (total * (1.0 / (2 * WIN + 1)) + EPSILON)
        for part in range(per_block):
            inside = inverse[part * bins : (part + 1) * bins]
            real = spec_buf[step % 2, seg, part * bins : (part + 1) * bins, :] * inside
            imag = spec_buf[step % 2, seg, BLOCK + part * bins : BLOCK + (part + 1) * bins, :]
            both = jnp.concatenate([real, imag * inside], axis=0).astype(BF16)
            sent_buf[block * per_block + part, seg * rows : (seg + 1) * rows, :] = both

    def piece_copy(number, seg):
        place = pl.ds(seg * rows, rows)
        return pltpu.make_async_remote_copy(
            src_ref=sent_buf.at[number, place],
            dst_ref=got_buf.at[me, place],
            send_sem=send_sem.at[number],
            recv_sem=recv_sem.at[me],
            device_id={"sta": home_of(number, group_count)},
            device_id_type=MESH,
        )

    def whiten(step):
        block = block_of(step)
        for seg in range(seg_count):
            whiten_segment(step, seg)

        @pl.when(step == 1)
        def _():
            for part in range(per_block):
                bulk_copy(block * per_block + part, me).start()

        @pl.when(step == 3)
        def _():
            base = jnp.where(upper, quarter, half)
            for part in range(quarter):
                bulk_copy(base + (me + part) % quarter, me).start()

        @pl.when(step >= 4)
        def _():
            for part in range(per_block):
                number = block * per_block + part

                @pl.when(number != mine)
                def _():
                    bulk_copy(number, me).start()

                @pl.when(number == mine)
                def _():
                    got_buf[me] = sent_buf[mine]

    for step in range(2):
        table_copy(step).wait()
    for seg in range(seg_count):
        strain_copies[seg].wait()
        if seg == 1:
            for step in range(2, 4):
                table_copy(step).start()
        transform_segment(0, seg)
        transform_segment(1, seg)
        whiten_segment(0, seg)
        for part in range(per_block):
            piece_copy(block_of(0) * per_block + part, seg).start()


    def body(step, carry):
        transform(step)
        whiten(step - 1)
        return carry

    lax.fori_loop(2, BLOCKS, body, 0)
    for step in range(1, group_count):
        index_copy(step).wait_recv()
    index_share().start()
    whiten(BLOCKS - 1)
    index_share().wait()

    one, zero = jnp.ones((channels, CHUNK), BF16), jnp.zeros((channels, CHUNK), BF16)
    other_mask = masks_ref[0, 0] ^ masks_ref[0, 1] ^ full_mask
    other_mask = jnp.bitwise_and(other_mask, full_mask)

    def index_of(group):
        return jnp.concatenate([index_buf[0, group], index_buf[1, group]], axis=1)

    def pick(source):
        block = got_buf[source]
        partner = full_mask - source
        listed = [
            index_of(source),
            index_of(partner),
            index_of(jnp.bitwise_xor(source, other_mask)),
        ]
        places = [near_buf.at[source], full_buf.at[partner], other_buf.at[source]]
        for chunk in range(chunks):
            for n in range(3):
                row = listed[n][4 * chunk + n : 4 * chunk + n + 1]
                chosen = dot(block, jnp.where(iota_buf[...] == row, one, zero))
                places[n][:, chunk * CHUNK : (chunk + 1) * CHUNK] = chosen.astype(BF16)

    def near_group(number, carry):
        source = near_base + (me + number) % half

        @pl.when(source != me)
        def _():
            bulk_copy(source, source).wait_recv()

        pick(source)
        return carry

    def far_group(number, carry):
        source = far_base + (mine - number // 2 + group_count) % quarter + quarter * (number % 2)
        bulk_copy(source, source).wait_recv()
        pick(source)
        return carry

    lax.fori_loop(0, half, near_group, 0)
    lax.fori_loop(0, half, far_group, 0)

    def part_of(shape, axis, size, number):
        return (lax.broadcasted_iota(jnp.int32, shape, axis) // size == number).astype(F32)

    per_tile = 128 // capacity
    group_tiles = group_count // per_tile
    half_tiles = group_tiles // 2
    lane = lax.broadcasted_iota(jnp.int32, (coefs, 128), 1) // capacity
    tall = jnp.concatenate([left_ref[...].astype(F32)] * per_tile, axis=0)
    widest = sum(
        pltpu.roll(tall, rows * i, 1) * (part_of(tall.shape, 0, 2 * coefs, i)) for i in range(per_tile)
    )
    wide_ref[...] = widest[:, : rows * per_tile].astype(BF16)

    def cross_of(group, lanes):
        peer = jnp.bitwise_xor(group, other_mask)
        real, imag = 0.0, 0.0
        for seg in range(seg_count):
            low = seg * rows
            a = near_buf[group, low : low + rows, lanes].astype(F32)
            b = full_buf[group, low : low + rows, lanes]
            b = (b + other_buf[peer, low : low + rows, lanes]).astype(F32)
            ar, ai, br, bi = a[:bins], a[bins:], b[:bins], b[bins:]
            real = real + (ar * br + ai * bi)
            imag = imag + (ai * br - ar * bi)
        return jnp.concatenate([real, imag], axis=0).astype(BF16)

    def tile_of(tile):
        found = [[] for _ in range(per_tile)]
        for chunk in range(chunks):
            lanes = slice(chunk * CHUNK, (chunk + 1) * CHUNK)
            cross = [cross_of(tile * per_tile + i, lanes) for i in range(per_tile)]
            both = dot(wide_ref[...], jnp.concatenate(cross, axis=0))
            for i in range(per_tile):
                part = both[2 * coefs * i : 2 * coefs * (i + 1)]
                found[i].append(part[:coefs] + part[coefs:])
        parts = [jnp.concatenate(f, axis=1) for f in found]
        blocks = []
        for owner_tile in range(slots // 128):
            cut = [p[:, owner_tile * 128 : (owner_tile + 1) * 128] for p in parts]
            for o in range(per_tile):
                block = cut[0] if o == 0 else pltpu.roll(cut[0], (128 - o * capacity) % 128, 1)
                for i in range(1, per_tile):
                    turned = cut[i]
                    if i != o:
                        turned = pltpu.roll(turned, ((i - o) * capacity) % 128, 1)
                    block = jnp.where(lane == i, turned, block)
                blocks.append(block)
        return blocks

    def part_copy(number):
        return pltpu.make_async_remote_copy(
            src_ref=part_buf.at[number],
            dst_ref=sum_in.at[number],
            send_sem=psend_sem.at[number],
            recv_sem=precv_sem.at[number],
            device_id={"tm": 1 - core},
            device_id_type=MESH,
        )

    stage_tiles = half_tiles // STAGES
    stage_width = stage_tiles * 128

    def lanes_of(side, stage):
        start = (STAGES * side + stage) * stage_width
        return pl.ds(pl.multiple_of(start, stage_width), stage_width)

    def slot_of(source, side, stage):
        return out_ref.at[source, :, lanes_of(side, stage)]

    def result_copy(number, stage, side):
        return pltpu.make_async_remote_copy(
            src_ref=res_buf.at[stage, number],
            dst_ref=slot_of(me, core, stage),
            send_sem=rsend_sem.at[stage],
            recv_sem=rrecv_sem.at[stage, side],
            device_id={"sta": number},
            device_id_type=MESH,
        )

    def arrived(stage, side, count):
        place = out_ref.at[pl.ds(0, count), :, lanes_of(core, stage)]
        return pltpu.make_async_remote_copy(
            src_ref=place,
            dst_ref=place,
            send_sem=rsend_sem.at[stage],
            recv_sem=rrecv_sem.at[stage, side],
            device_id={"sta": far_base},
            device_id_type=MESH,
        )

    def forward_copy(base, count, side, stage):
        place = out_ref.at[pl.ds(base, count), :, lanes_of(side, stage)]
        return pltpu.make_async_remote_copy(
            src_ref=place,
            dst_ref=place,
            send_sem=fsend_sem.at[stage],
            recv_sem=frecv_sem.at[stage],
            device_id={"tm": 1 - core},
            device_id_type=MESH,
        )

    def own_copy(stage):
        return pltpu.make_async_copy(
            res_buf.at[stage, me], slot_of(me, core, stage), own_sem.at[stage]
        )

    def stage_of(stage, carry):
        def theirs(number, carry):
            blocks = tile_of((1 - core) * half_tiles + number)
            for o in range(group_count):
                part_buf[number, o] = blocks[o].astype(BF16)
            part_copy(number).start()
            return carry

        lax.fori_loop(stage * stage_tiles, (stage + 1) * stage_tiles, theirs, 0)
        for n in range(stage_tiles):
            number = stage * stage_tiles + n
            blocks = tile_of(core * half_tiles + number)
            part_copy(number).wait_recv()
            for o in range(group_count):
                total = blocks[o] + sum_in[number, o].astype(F32)
                res_buf[stage, o, :, n * 128 : (n + 1) * 128] = total.astype(BF16)
        for step in range(half):
            result_copy(far_base + (me + step) % half, stage, 1).start()
        own_copy(stage).start()
        for step in range(1, half):
            result_copy(near_base + (me + step) % half, stage, 0).start()
        return carry

    lax.fori_loop(0, STAGES, stage_of, 0)

    for step in range(1, group_count):
        bulk_copy((mine + step) % group_count, me).wait_send()
        index_copy(step).wait_send()
    for number in range(half_tiles):
        part_copy(number).wait_send()
    for stage in range(STAGES):
        own_copy(stage).wait()
        arrived(stage, 0, half - 1).wait_recv()
        forward_copy(near_base, half, core, stage).start()
        arrived(stage, 1, half).wait_recv()
        forward_copy(far_base, half, core, stage).start()
    for stage in range(STAGES):
        arrived(stage, 1, group_count - 1).wait_send()
    for stage in range(STAGES):
        forward_copy(0, group_count, core, stage).wait_send()
        forward_copy(0, group_count, 1 - core, stage).wait_recv()


def per_device(strain, masks, pair_local, pair_remote, owner):
    group_count = lax.axis_size("sta")
    time_count = lax.axis_size("tm")
    seg_count = strain.shape[0] // SEG_LEN
    channels = strain.shape[1]
    round_count, pair_count = pair_local.shape
    capacity = max(2, 2 * round_count * pair_count // group_count)
    slots = group_count * capacity
    bins = FREQS // group_count
    rows = seg_count * 2 * bins
    count = min(COEFS, 2 * bins)
    norm_scale = 1.0 / math.sqrt(seg_count * time_count * FREQS)
    left, right = inverse_factors(group_count, norm_scale)
    order = [slice_of(group, group_count) for group in range(group_count)]
    right = right.reshape(group_count, count, LAGS)[np.array(order)].reshape(-1, LAGS)
    half_tiles = slots // 256
    pairs = round_count * pair_count
    lists = owner.reshape(1, pairs)
    for array in (pair_local, pair_remote, masks[None, :]):
        array = jnp.pad(array, ((0, 0), (0, pairs - array.shape[1])))
        lists = jnp.concatenate([lists, array])
    dma = pltpu.SemaphoreType.DMA
    vmem = pl.BlockSpec(memory_space=pltpu.VMEM)
    coefs = pl.pallas_call(
        functools.partial(main_kernel, group_count, capacity, seg_count, pair_local.shape),
        out_shape=jax.ShapeDtypeStruct((group_count, count, slots), BF16),
        in_specs=[pl.BlockSpec(memory_space=pl.ANY)] * 2 + [vmem],
        out_specs=vmem,
        scratch_shapes=[
            pltpu.VMEM(((seg_count - 1) * SEG_LEN + SEG_PAD, channels), BF16),
            pltpu.VMEM((BLOCKS, 2 * BLOCK, SEG_PAD), BF16),
            pltpu.VMEM((2 * count, 128), BF16),
            pltpu.SMEM((1, round_count * pair_count), jnp.int32),
            pltpu.VMEM((2 * count * (128 // capacity), 2 * bins * (128 // capacity)), BF16),
            pltpu.VMEM((2, seg_count, 2 * BLOCK, channels), F32),
            pltpu.VMEM((seg_count, (BLOCKS + 2) * BLOCK, channels), BF16),
            pltpu.VMEM((seg_count, (BLOCKS + 2) * BLOCK, channels), BF16),
            pltpu.VMEM((channels, CHUNK), BF16),
            pltpu.VMEM((group_count, rows, channels), BF16),
            pltpu.VMEM((group_count, rows, channels), BF16),
            pltpu.VMEM((group_count, rows, slots), BF16),
            pltpu.VMEM((group_count, rows, slots), BF16),
            pltpu.VMEM((group_count, rows, slots), BF16),
            pltpu.VMEM((16, CHUNK // 2), BF16),
            pltpu.VMEM((2, group_count, 16, CHUNK // 2), BF16),
            pltpu.VMEM((half_tiles, group_count, count, 128), BF16),
            pltpu.VMEM((half_tiles, group_count, count, 128), BF16),
            pltpu.VMEM((STAGES, group_count, count, half_tiles * 128 // STAGES), BF16),
            dma((2,)),
            dma((seg_count,)),
            dma((BLOCKS,)),
            dma((group_count,)),
            dma((group_count,)),
            dma((group_count,)),
            dma((group_count,)),
            dma((half_tiles,)),
            dma((half_tiles,)),
            dma((STAGES,)),
            dma((STAGES, 2)),
            dma((STAGES,)),
            dma((STAGES,)),
            dma((STAGES,)),
        ],
        compiler_params=pltpu.CompilerParams(
            collective_id=0, has_side_effects=True, vmem_limit_bytes=48 * 1024 * 1024
        ),
    )(strain, jnp.asarray(tables(left)), lists)
    width = LAGS // time_count
    mine = lax.dynamic_slice_in_dim(
        jnp.asarray(right), lax.axis_index("tm") * width, width, axis=1
    )
    coefs = coefs.reshape(group_count * count, slots)
    return jnp.einsum("cs,cl->sl", coefs, mine, preferred_element_type=F32)


def solution(mesh):
    placed = (P("tm", "sta"), P(), P(None, "sta"), P(None, "sta"), P("sta", None))
    return jax.shard_map(
        per_device, mesh=mesh, in_specs=placed, out_specs=P("sta", "tm"), check_vma=False
    )
```
